128 devices in a mesh: row: 8 (over y, core), col: 16 (over z, x).
Axes of the slice: x: 4, y: 4, z: 4, core: 2. Of those that a mesh axis runs over, the one named last changes fastest.
Arguments:
- object_field: float32 [2, 2048, 4096], P(None, 'row', 'col'), may hold values from -0.4 to 0.4
- probe: float32 [2, 256, 256], replicated, may hold values from -8 to 8
- positions: int32 [2048, 2], P(('row', 'col')), may hold values from 0 to 3840, as said below
- amplitudes: bfloat16 [2048, 256, 256], P(('row', 'col')), may hold values from 0.25 to 2.5
- live: int32 [128], P(('row', 'col')), may hold values from 8 to 16, as said below
- kernel_first: float32 [2, 3, 3], replicated, may hold values from -4 to 4
- kernel_second: float32 [2, 3, 3], replicated, may hold values from -4 to 4
Outputs:
- object_out: float32 [2, 2048, 4096], P(None, 'row', 'col')
- probe_out: float32 [2, 256, 256], replicated
The draws below stay inside these ranges and needn't reach their ends.
Inputs may be any that keep to these rules, and one draw needn't show every extreme that they name: `positions`: slot s is owned by device s // 16 of the row+col axis (row slowest); its window's top-left pixel lies in that device's tile (256 x 256), except that rows are clamped to at most 1792 and columns to at most 3840, so every window lies inside the object. `live`: some device uses all 16 slots; every device uses at least half of them.
All inputs are finite; a program needn't handle non-finite values.
Results may differ from the reference program's by a relative error of at most 0.006.
The reference program's roundings to bfloat16 on the way count: a program that leaves them out, or rounds other values in their place, can miss the bound.
Values sent between devices are 32-bit elements; how exact they have to be, the bound alone decides.
A program may use at most 128 MiB of HBM per device.

```python
import math
import jax
import jax.numpy as jnp
from jax import lax

W = 256
TR = 256
TC = 256
POS_DEV = 16
ITERS = 2
NR = 2048
NC = 4096
TOTAL_POS = 2048
N_COL = 16
DEVICES = 128


def draw_positions(key, part):
    key = jax.random.fold_in(key, 11)
    key_rows, key_cols = jax.random.split(key)
    slots = jnp.arange(TOTAL_POS, dtype=jnp.int32)
    owner = slots // POS_DEV
    block_row = owner // N_COL
    block_col = owner % N_COL
    rows = block_row * TR + jax.random.randint(key_rows, (TOTAL_POS,), 0, TR, dtype=jnp.int32)
    cols = block_col * TC + jax.random.randint(key_cols, (TOTAL_POS,), 0, TC, dtype=jnp.int32)
    rows = jnp.minimum(rows, NR - W)
    cols = jnp.minimum(cols, NC - W)
    return jnp.stack([rows, cols], axis=1).astype(jnp.int32)


def draw_live(key, part):
    key = jax.random.fold_in(key, 23)
    key_counts, key_full = jax.random.split(key)
    counts = jax.random.randint(key_counts, (DEVICES,), POS_DEV // 2, POS_DEV + 1, dtype=jnp.int32)
    chosen = jax.random.randint(key_full, (), 0, DEVICES, dtype=jnp.int32)
    index = jnp.arange(DEVICES, dtype=jnp.int32)
    return jnp.where(index == chosen, POS_DEV, counts).astype(jnp.int32)


def level_of(stream_key, shape, cuts, low, largest):
    factor_of, own = 1.0, jax.random.fold_in(stream_key, 6)
    for axis_at, shards_of in cuts:
        heights = jnp.exp(jax.random.uniform(jax.random.fold_in(own, axis_at), (shards_of,), jnp.float32, low / len(cuts), largest / len(cuts)))
        factor_of = factor_of * jnp.repeat(heights, shape[axis_at] // shards_of).reshape([-1 if axis == axis_at else 1 for axis in range(len(shape))])
    return factor_of


def normal_values(key, extent, width, reach, kind=jnp.bfloat16):
    entries = jax.random.normal(key, extent, jnp.float32) * width
    return jnp.minimum(jnp.maximum(entries, -reach), reach).astype(kind)


def setup_inputs(seed: int = 0) -> dict:
    keys = jax.random.split(jax.random.key(seed), 8)
    return {
        "object_field": jnp.clip(jax.random.uniform(keys[0], (2, NR, NC), jnp.float32, -0.4, 0.4) * level_of(keys[0], (2, NR, NC), ((1, 8), (2, 16)), -0.4, 0.0), -0.4, 0.4),
        "probe": normal_values(keys[1], (2, W, W), 1.875, 8.0, jnp.float32),
        "positions": draw_positions(jax.random.fold_in(keys[7], 71), 0),
        "amplitudes": jnp.clip(jnp.exp(math.log(2.5) - 2.3025851 * jax.random.uniform(keys[3], (TOTAL_POS, W, W), jnp.float32) ** level_of(keys[3], (TOTAL_POS, W, W), ((0, 128),), -0.2, 0.2)), 0.25, 2.5).astype(jnp.bfloat16),
        "live": draw_live(jax.random.fold_in(keys[7], 71), 0),
        "kernel_first": normal_values(keys[5], (ITERS, 3, 3), 0.35, 4.0, jnp.float32),
        "kernel_second": normal_values(keys[6], (ITERS, 3, 3), 0.35, 4.0, jnp.float32),
    }


def dft_tables(length):
    steps = jnp.arange(length, dtype=jnp.int32)
    product = steps[:, None] * steps[None, :] % length
    angle = product.astype(jnp.float32) * (2.0 * math.pi / length)
    scale = 1.0 / math.sqrt(length)
    return ((jnp.cos(angle) * scale).astype(jnp.bfloat16), (-jnp.sin(angle) * scale).astype(jnp.bfloat16))

def matmul(left, right):
    return jnp.dot(left.astype(jnp.float32), right.astype(jnp.float32), preferred_element_type=jnp.float32)

def transform(table_re, table_im, value_re, value_im):
    half_re = (matmul(table_re, value_re) - matmul(table_im, value_im)).astype(jnp.bfloat16)
    half_im = (matmul(table_re, value_im) + matmul(table_im, value_re)).astype(jnp.bfloat16)
    out_re = matmul(half_re, table_re) - matmul(half_im, table_im)
    out_im = matmul(half_re, table_im) + matmul(half_im, table_re)
    return (out_re, out_im)

def position_terms(window, probe, amp, weight, table_re, table_im):
    exit_re = (probe[0] * window[0] - probe[1] * window[1]).astype(jnp.bfloat16)
    exit_im = (probe[0] * window[1] + probe[1] * window[0]).astype(jnp.bfloat16)
    spec_re, spec_im = transform(table_re, table_im, exit_re, exit_im)
    magnitude = jnp.sqrt(spec_re * spec_re + spec_im * spec_im)
    factor = amp.astype(jnp.float32) / jnp.maximum(magnitude, 0.25)
    diff_re = (factor * spec_re - spec_re).astype(jnp.bfloat16)
    diff_im = (factor * spec_im - spec_im).astype(jnp.bfloat16)
    change_re, change_im = transform(table_re, -table_im, diff_re, diff_im)
    change_re = change_re * weight
    change_im = change_im * weight
    object_term = jnp.stack([probe[0] * change_re + probe[1] * change_im, probe[0] * change_im - probe[1] * change_re])
    probe_term = jnp.stack([window[0] * change_re + window[1] * change_im, window[0] * change_im - window[1] * change_re])
    return (object_term, probe_term)

def correlate(field, kernel):
    padded = jnp.pad(field, 1)
    rows, cols = field.shape
    total = jnp.zeros_like(field)
    for shift_a in range(3):
        for shift_b in range(3):
            total = total + kernel[shift_a, shift_b] * padded[shift_a:shift_a + rows, shift_b:shift_b + cols]
    return total

def reference(object_field, probe, positions, amplitudes, live, kernel_first, kernel_second):
    table_re, table_im = dft_tables(W)
    slots = jnp.arange(TOTAL_POS, dtype=jnp.int32)
    counts = live[slots // POS_DEV]
    weights = (slots % POS_DEV < counts).astype(jnp.float32)
    zero = jnp.zeros((), jnp.int32)
    for step in range(ITERS):
        current = object_field
        current_probe = probe

        def visit(carry, item):
            accum, probe_accum = carry
            offset, amp, weight = item
            start = (zero, offset[0], offset[1])
            window = lax.dynamic_slice(current, start, (2, W, W))
            object_term, probe_term = position_terms(window, current_probe, amp, weight, table_re, table_im)
            placed = lax.dynamic_slice(accum, start, (2, W, W)) + object_term
            accum = lax.dynamic_update_slice(accum, placed, start)
            return ((accum, probe_accum + probe_term), None)
        init = (jnp.zeros_like(current), jnp.zeros_like(current_probe))
        (accum, probe_accum), _ = lax.scan(visit, init, (positions, amplitudes, weights))
        stepped = current + accum / POS_DEV
        probe = current_probe + 2.0 * probe_accum / math.sqrt(TOTAL_POS)
        real_part = stepped[0] + jnp.tanh(correlate(stepped[1], kernel_first[step]))
        imag_part = stepped[1] + jnp.tanh(correlate(real_part, kernel_second[step]))
        object_field = jnp.stack([real_part, imag_part])
    return (object_field, probe)
```

```python
import functools
import math

import jax
import jax.numpy as jnp
import ml_dtypes
import numpy as np
from jax import lax
from jax.experimental import pallas as pl
from jax.experimental.pallas import tpu as pltpu
from jax.sharding import PartitionSpec as P

W = 256
LANE = 128
ROWS = 8
COLS = 16
CHUNKS = 4
CH = W // CHUNKS
MESH = pl.DeviceIdType.MESH
F32 = jnp.float32
BF16 = jnp.bfloat16


def dft_tables():
    steps = np.arange(W)
    product = (steps[:, None] * steps[None, :]) % W
    angle = product.astype(np.float32) * np.float32(2.0 * math.pi / W)
    scale = np.float32(1.0 / math.sqrt(W))
    fr = (np.cos(angle) * scale).astype(ml_dtypes.bfloat16)
    fi = (-np.sin(angle) * scale).astype(ml_dtypes.bfloat16)
    left = np.block([[fr, -fi], [fi, fr]])
    return left, np.ascontiguousarray(left.T)


def dot(a, b):
    return jnp.dot(a, b, preferred_element_type=F32)


def window_kernel(pos, live, ext, probe, amps, left, right, acc, pacc, win, ebuf, dbuf, cbuf, amp_v, sems):
    slots = amps.shape[0]
    group = 2

    def amp_copy(s):
        return pltpu.make_async_copy(amps.at[s], amp_v.at[s], sems.at[s])

    for s in range(slots):
        amp_copy(s).start()

    def zero(i, _):
        rows = pl.ds(pl.multiple_of(i * 8, 8), 8)
        for part in range(2):
            for t in range(4):
                acc[part, t, rows, :] = jnp.zeros((8, LANE), F32)
        return 0

    lax.fori_loop(0, 64, zero, 0)

    def zero_probe(i, _):
        pacc[pl.ds(pl.multiple_of(i * 64, 64), 64), :] = jnp.zeros((64, LANE), F32)
        return 0

    lax.fori_loop(0, 16, zero_probe, 0)
    lane = lax.broadcasted_iota(jnp.int32, (32, LANE), 1)

    def place_of(s):
        r = pos[s, 0]
        c = pos[s, 1]
        q = c // LANE
        return r, q, c - q * LANE

    def step(p, _):
        for g in range(group):
            r, q, sh = place_of(p * group + g)

            def form(i, _):
                o = pl.multiple_of(i * 32, 32)
                rows = pl.ds(o, 32)
                keep = lane < LANE - sh
                w = []
                for part in range(2):
                    cuts = [pltpu.roll(ext[part, q + t, pl.ds(r + o, 32), :], LANE - sh, 1) for t in range(3)]
                    w.append([jnp.where(keep, cuts[t], cuts[t + 1]) for t in range(2)])
                for t in range(2):
                    cols = slice(t * LANE, (t + 1) * LANE)
                    win[g, 0, rows, cols] = w[0][t]
                    win[g, 1, rows, cols] = w[1][t]
                    pr = probe[pl.ds(t * W + o, 32), :]
                    pi = probe[pl.ds(2 * W + t * W + o, 32), :]
                    ebuf[g, rows, cols] = (pr * w[0][t] - pi * w[1][t]).astype(BF16)
                    ebuf[g, pl.ds(o + W, 32), cols] = (pr * w[1][t] + pi * w[0][t]).astype(BF16)
                return 0

            lax.fori_loop(0, 8, form, 0, unroll=True)
        for g in range(group):
            s = p * group + g
            half = dot(left[...], ebuf[g]).astype(BF16)
            spec = dot(jnp.concatenate([half[:W], half[W:]], axis=1), right[...])
            amp_copy(s).wait()
            amp = amp_v[s].astype(F32)
            sr, si = spec[:, :W], spec[:, W:]
            f = amp * lax.rsqrt(jnp.maximum(sr * sr + si * si, 0.0625)) - 1.0
            f = jnp.where(s < live[0], f, 0.0)
            dbuf[g, :W] = (f * sr).astype(BF16)
            dbuf[g, W:] = (f * si).astype(BF16)
        for g in range(group):
            back = dot(right[...], dbuf[g]).astype(BF16)
            cbuf[g] = dot(jnp.concatenate([back[:W], back[W:]], axis=1), left[...])
        for g in range(group):
            r, q, sh = place_of(p * group + g)

            def put(i, _):
                o = pl.multiple_of(i * 32, 32)
                rows = pl.ds(o, 32)
                keep = lane >= sh
                terms = [[], []]
                for t in range(2):
                    cols = slice(t * LANE, (t + 1) * LANE)
                    at_re = pl.ds(t * W + o, 32)
                    at_im = pl.ds(2 * W + t * W + o, 32)
                    pr = probe[at_re, :]
                    pi = probe[at_im, :]
                    cr = cbuf[g, rows, cols]
                    ci = cbuf[g, rows, W + t * LANE : W + (t + 1) * LANE]
                    wr = win[g, 0, rows, cols]
                    wi = win[g, 1, rows, cols]
                    pacc[at_re, :] += wr * cr + wi * ci
                    pacc[at_im, :] += wr * ci - wi * cr
                    terms[0].append(pltpu.roll(pr * cr + pi * ci, sh, 1))
                    terms[1].append(pltpu.roll(pr * ci - pi * cr, sh, 1))
                at = pl.ds(r + o, 32)
                for part in range(2):
                    a, b = terms[part]
                    acc[part, q, at, :] += jnp.where(keep, a, 0.0)
                    acc[part, q + 1, at, :] += jnp.where(keep, b, a)
                    acc[part, q + 2, at, :] += jnp.where(keep, 0.0, b)
                return 0

            lax.fori_loop(0, 8, put, 0, unroll=True)
        return 0

    lax.fori_loop(0, slots // group, step, 0)


VM = pl.BlockSpec(memory_space=pltpu.VMEM)
SM = pl.BlockSpec(memory_space=pltpu.SMEM)
ANY = pl.BlockSpec(memory_space=pl.ANY)
EXT = jax.ShapeDtypeStruct((2, 4, 2 * W, LANE), F32)
FLAT = jax.ShapeDtypeStruct((4 * W, LANE), F32)
TILE = jax.ShapeDtypeStruct((2, 2, W, LANE), F32)
DMA = pltpu.SemaphoreType.DMA


def window_call(local, live, ext, probe, amps, left, right):
    slots = amps.shape[0]
    group = 2
    return pl.pallas_call(
        window_kernel,
        out_shape=(EXT, FLAT),
        in_specs=[SM, SM, VM, VM, ANY, VM, VM],
        out_specs=(VM, VM),
        scratch_shapes=[
            pltpu.VMEM((group, 2, W, W), F32),
            pltpu.VMEM((group, 2 * W, W), BF16),
            pltpu.VMEM((group, 2 * W, W), BF16),
            pltpu.VMEM((group, W, 2 * W), F32),
            pltpu.VMEM((slots, W, W), BF16),
            DMA((slots,)),
        ],
        compiler_params=pltpu.CompilerParams(vmem_limit_bytes=48 * 2**20),
        name="windows",
    )(local, live, ext, probe, amps, left, right)


def remote(src, dst, send, recv, to):
    return pltpu.make_async_remote_copy(
        src_ref=src, dst_ref=dst, send_sem=send, recv_sem=recv, device_id=to, device_id_type=MESH
    )


def where_am_i():
    row = lax.axis_index("row")
    col = lax.axis_index("col")
    up = (lax.rem(row + ROWS - 1, ROWS), col)
    down = (lax.rem(row + 1, ROWS), col)
    west = (row, lax.rem(col + COLS - 1, COLS))
    east = (row, lax.rem(col + 1, COLS))
    return row, col, up, down, west, east


def greet(targets):
    barrier = pltpu.get_barrier_semaphore()
    for target in targets:
        pl.semaphore_signal(barrier, inc=1, device_id=target, device_id_type=MESH)
    pl.semaphore_wait(barrier, len(targets))


def chunk(k, base=0):
    return pl.ds(base + k * CH, CH)


def halo_start(ext, send, recv, west, up):
    own = slice(0, 2)
    far = slice(2, 4)
    to_west = [
        remote(ext.at[:, own, chunk(k), :], ext.at[:, far, chunk(k), :], send.at[k], recv.at[k], west)
        for k in range(CHUNKS)
    ]
    to_up = remote(
        ext.at[:, own, pl.ds(0, W), :], ext.at[:, own, pl.ds(W, W), :], send.at[CHUNKS], recv.at[CHUNKS], up
    )
    onward = [
        remote(
            ext.at[:, far, chunk(k), :],
            ext.at[:, far, chunk(k, W), :],
            send.at[CHUNKS + 1 + k],
            recv.at[CHUNKS + 1 + k],
            up,
        )
        for k in range(CHUNKS)
    ]
    for copy in to_west:
        copy.start()
    to_up.start()
    return to_west, to_up, onward


def halo_finish(copies):
    to_west, to_up, onward = copies
    for first, second in zip(to_west, onward):
        first.wait_recv()
        second.start()
    to_up.wait_recv()
    for copy in onward:
        copy.wait_recv()
    for copy in [*to_west, to_up, *onward]:
        copy.wait_send()


HALO_SEMS = 2 * CHUNKS + 1


def halo_kernel(obj, probe, ext, flat, send, recv):
    row, col, up, down, west, east = where_am_i()

    def lay(i, _):
        rows = pl.ds(pl.multiple_of(i * 32, 32), 32)
        for part in range(2):
            for t in range(2):
                ext[part, t, rows, :] = obj[part, rows, t * LANE : (t + 1) * LANE]
        return 0

    lax.fori_loop(0, W // 32, lay, 0)
    greet([up, down, west, east])
    copies = halo_start(ext, send, recv, west, up)

    def lay_probe(i, _):
        o = pl.multiple_of(i * 32, 32)
        for part in range(2):
            for t in range(2):
                flat[pl.ds((part * 2 + t) * W + o, 32), :] = probe[part, pl.ds(o, 32), t * LANE : (t + 1) * LANE]
        return 0

    lax.fori_loop(0, W // 32, lay_probe, 0)
    halo_finish(copies)


def halo_call(obj, probe):
    return pl.pallas_call(
        halo_kernel,
        out_shape=(EXT, FLAT),
        in_specs=[VM, VM],
        out_specs=(VM, VM),
        scratch_shapes=[DMA((HALO_SEMS,)), DMA((HALO_SEMS,))],
        compiler_params=pltpu.CompilerParams(
            collective_id=0, has_side_effects=True, vmem_limit_bytes=48 * 2**20
        ),
        name="first_halo",
    )(obj, probe)


TOP = 16
FRAME = W + 2 * TOP


def correlate_block(v, o, count, kernel, slabs, lane):
    sums = {}
    wanted = range(slabs[0] - 1, slabs[-1] + 2)
    for t in wanted:
        if t < 0 or t > 3:
            continue
        above, here, below = (v(t, o + a) for a in (-1, 0, 1))
        sums[t] = [above * kernel[0, b] + here * kernel[1, b] + below * kernel[2, b] for b in range(3)]
    out = []
    for t in slabs:
        before = pltpu.roll(sums[t][0], 1, 1)
        if t > 0:
            before = jnp.where(lane == 0, pltpu.roll(sums[t - 1][0], 1, 1), before)
        after = pltpu.roll(sums[t][2], LANE - 1, 1)
        if t < 3:
            after = jnp.where(lane == LANE - 1, pltpu.roll(sums[t + 1][2], LANE - 1, 1), after)
        out.append(sums[t][1] + before + after)
    return out


def update_kernel(
    last, acc, ext_old, pacc, flat_old, kf, ks, ext, flat,
    from_up, from_west, onward, rim_out, rim_in, frame, real,
    p1, h1, p2, h2, p3,
    y_send, y_recv, x_send, x_recv, rim_send, rim_recv, h_send, h_recv,
    a_send, a_recv, b_send, b_recv, c_send, c_recv, d_send, d_recv,
):
    row, col, up, down, west, east = where_am_i()
    core = lax.rem(row, 2)
    y = row // 2
    mate = (row + 1 - 2 * core, col)
    beyond = (lax.rem(row + ROWS - 1 + 2 * core, ROWS), col)
    in_y = [(lax.rem(row + 2 * d, ROWS), col) for d in range(1, 4)]
    in_col = [(row, lax.rem(col + d, COLS)) for d in range(1, COLS)]
    greet([mate, beyond, *in_y, *in_col])

    y_copies = [
        remote(acc.at[:, pl.ds(2, 2), chunk(k, W), :], from_up.at[:, pl.ds(2, 2), chunk(k), :], y_send.at[k], y_recv.at[k], down)
        for k in range(CHUNKS)
    ]
    y_copies.append(
        remote(acc.at[:, pl.ds(0, 2), pl.ds(W, W), :], from_up.at[:, pl.ds(0, 2), :, :], y_send.at[CHUNKS], y_recv.at[CHUNKS], down)
    )
    for copy in y_copies:
        copy.start()

    mine = pl.multiple_of(core * 512, 512)
    other = pl.multiple_of(512 - core * 512, 512)
    a_copies = [remote(pacc.at[pl.ds(other, 512), :], p1, a_send.at[0], a_recv.at[0], mate)]
    a_copies[0].start()

    x_copies = []
    for k in range(CHUNKS):
        y_copies[k].wait_recv()

        def join(i, _):
            o = pl.multiple_of(i * 16, 16)
            for part in range(2):
                for t in range(2):
                    onward[part, t, pl.ds(k * CH + o, 16), :] = (
                        acc[part, 2 + t, pl.ds(k * CH + o, 16), :] + from_up[part, 2 + t, pl.ds(k * CH + o, 16), :]
                    )
            return 0

        lax.fori_loop(0, CH // 16, join, 0)
        copy = remote(onward.at[:, :, chunk(k), :], from_west.at[:, :, chunk(k), :], x_send.at[k], x_recv.at[k], east)
        copy.start()
        x_copies.append(copy)

    a_copies[0].wait_recv()

    def join_half(i, _):
        o = pl.multiple_of(i * 64, 64)
        h1[pl.ds(o, 64), :] = pacc[pl.ds(mine + o, 64), :] + p1[pl.ds(o, 64), :]
        return 0

    lax.fori_loop(0, 8, join_half, 0)
    b_copies = []
    for d in range(1, 4):
        block = pl.multiple_of(lax.rem(y + d, 4) * LANE, LANE)
        b_copies.append(remote(h1.at[pl.ds(block, LANE), :], p2.at[d - 1], b_send.at[d - 1], b_recv.at[d - 1], in_y[d - 1]))
    for copy in b_copies:
        copy.start()

    for t in range(4):
        for part in range(2):
            frame[part, t, pl.ds(0, 8), :] = jnp.zeros((8, LANE), F32)
            frame[part, t, pl.ds(FRAME - 8, 8), :] = jnp.zeros((8, LANE), F32)

    def step_rows(k):
        def add(i, _):
            o = pl.multiple_of(k * CH + i * 16, 16)
            rows = pl.ds(o, 16)
            for part in range(2):
                for t in range(2):
                    total = acc[part, t, rows, :] + from_up[part, t, rows, :] + from_west[part, t, rows, :]
                    frame[part, 1 + t, pl.ds(TOP + o, 16), :] = ext_old[part, t, rows, :] + total * (1.0 / 16.0)
            return 0

        lax.fori_loop(0, CH // 16, add, 0)

    y_copies[CHUNKS].wait_recv()
    for k in range(CHUNKS // 2):
        x_copies[k].wait_recv()
        step_rows(k)

    for copy in b_copies:
        copy.wait_recv()
    here = pl.multiple_of(y * LANE, LANE)
    h2[...] = h1[pl.ds(here, LANE), :] + p2[0] + p2[1] + p2[2]
    c_copies = []
    for d in range(1, COLS):
        block = pl.multiple_of(lax.rem(col + d, COLS) * 8, 8)
        c_copies.append(remote(h2.at[pl.ds(block, 8), :], p3.at[d], c_send.at[d], c_recv.at[d], in_col[d - 1]))
    for copy in c_copies:
        copy.start()

    for k in range(CHUNKS // 2, CHUNKS):
        x_copies[k].wait_recv()
        step_rows(k)

    for part in range(2):
        rim_out[0, part, :, :] = frame[part, 1, pl.ds(TOP, W), :].T[:8, :]
        rim_out[1, part, :, :] = frame[part, 2, pl.ds(TOP, W), :].T[LANE - 8 :, :]
    rims = [
        remote(rim_out.at[0], rim_in.at[0], rim_send.at[0], rim_recv.at[0], west),
        remote(rim_out.at[1], rim_in.at[1], rim_send.at[1], rim_recv.at[1], east),
    ]
    rims[0].start()
    rims[1].start()

    for copy in c_copies:
        copy.wait_recv()
    own = pl.multiple_of(col * 8, 8)
    total = h2[pl.ds(own, 8), :]
    for d in range(1, COLS):
        total = total + p3[d]
    piece = pl.multiple_of(core * 512 + y * LANE + col * 8, 8)
    flat[pl.ds(piece, 8), :] = flat_old[pl.ds(piece, 8), :] + total * (2.0 / math.sqrt(2048.0))
    d_copies = []
    for d in range(1, COLS):
        d_copies.append(
            remote(flat.at[pl.ds(piece, 8), :], flat.at[pl.ds(piece, 8), :], d_send.at[d], d_recv.at[d], in_col[d - 1])
        )
    for copy in d_copies:
        copy.start()

    rims[0].wait_recv()
    rims[1].wait_recv()
    blank = jnp.zeros((LANE - 8, W), F32)
    for part in range(2):
        right_rim = jnp.where(col < COLS - 1, rim_in[0, part, :, :], 0.0)
        left_rim = jnp.where(col > 0, rim_in[1, part, :, :], 0.0)
        frame[part, 3, pl.ds(TOP, W), :] = jnp.concatenate([right_rim, blank], axis=0).T
        frame[part, 0, pl.ds(TOP, W), :] = jnp.concatenate([blank, left_rim], axis=0).T
    rows_out = [
        remote(frame.at[:, :, pl.ds(TOP, 8), :], frame.at[:, :, pl.ds(TOP + W, 8), :], rim_send.at[2], rim_recv.at[2], up),
        remote(frame.at[:, :, pl.ds(TOP + W - 8, 8), :], frame.at[:, :, pl.ds(TOP - 8, 8), :], rim_send.at[3], rim_recv.at[3], down),
    ]
    rows_out[0].start()
    rows_out[1].start()

    def gathered(first, count, send, recv, to):
        return remote(flat.at[pl.ds(first, count), :], flat.at[pl.ds(first, count), :], send, recv, to)

    for copy in d_copies:
        copy.wait_recv()
    quarter = pl.multiple_of(core * 512 + y * LANE, LANE)
    for d in range(1, 4):
        b_copies.append(gathered(quarter, LANE, b_send.at[2 + d], b_recv.at[2 + d], in_y[d - 1]))
        b_copies[-1].start()

    rows_out[0].wait_recv()
    rows_out[1].wait_recv()
    for part in range(2):
        for t in range(4):
            top = pl.ds(TOP - 8, 8)
            low = pl.ds(TOP + W, 8)
            frame[part, t, top, :] = jnp.where(row > 0, frame[part, t, top, :], 0.0)
            frame[part, t, low, :] = jnp.where(row < ROWS - 1, frame[part, t, low, :], 0.0)

    lane8 = lax.broadcasted_iota(jnp.int32, (8, LANE), 1)
    lane16 = lax.broadcasted_iota(jnp.int32, (16, LANE), 1)
    west_on = (col > 0).astype(F32)
    east_on = (col < COLS - 1).astype(F32)

    def first(i, _):
        o = pl.multiple_of(8 + i * 8, 8)
        parts = correlate_block(lambda t, at: frame[1, t, pl.ds(at, 8), :], o, 8, kf, range(4), lane8)
        keep_row = jnp.where(i == 0, (row > 0).astype(F32), jnp.where(i == 33, (row < ROWS - 1).astype(F32), 1.0))
        for t in range(4):
            value = frame[0, t, pl.ds(o, 8), :] + jnp.tanh(parts[t])
            keep = keep_row
            if t == 0:
                keep = keep * west_on
            if t == 3:
                keep = keep * east_on
            real[t, pl.ds(o, 8), :] = value * keep
        return 0

    lax.fori_loop(0, 34, first, 0)

    def second(i, _):
        o = pl.multiple_of(TOP + i * 16, 16)
        at = pl.ds(pl.multiple_of(i * 16, 16), 16)
        parts = correlate_block(lambda t, a: real[t, pl.ds(a, 16), :], o, 16, ks, range(1, 3), lane16)
        for t in range(2):
            ext[0, t, at, :] = real[1 + t, pl.ds(o, 16), :]
            ext[1, t, at, :] = frame[1, 1 + t, pl.ds(o, 16), :] + jnp.tanh(parts[t])
        return 0

    lax.fori_loop(0, 16, second, 0)

    if not last:
        copies = halo_start(ext, h_send, h_recv, west, up)

    for copy in b_copies[3:]:
        copy.wait_recv()
    a_copies.append(gathered(mine, 512, a_send.at[1], a_recv.at[1], mate))
    a_copies[1].start()
    if not last:
        halo_finish(copies)
    a_copies[1].wait_recv()
    for copy in [*y_copies, *x_copies, *a_copies, *b_copies, *c_copies, *d_copies, *rims, *rows_out]:
        copy.wait_send()


def update_call(last, acc, ext, pacc, flat, kf, ks):
    return pl.pallas_call(
        functools.partial(update_kernel, last),
        out_shape=(TILE if last else EXT, FLAT),
        in_specs=[VM, VM, VM, VM, SM, SM],
        out_specs=(VM, VM),
        scratch_shapes=[
            pltpu.VMEM((2, 4, W, LANE), F32),
            pltpu.VMEM((2, 2, W, LANE), F32),
            pltpu.VMEM((2, 2, W, LANE), F32),
            pltpu.VMEM((2, 2, 8, W), F32),
            pltpu.VMEM((2, 2, 8, W), F32),
            pltpu.VMEM((2, 4, FRAME, LANE), F32),
            pltpu.VMEM((4, FRAME, LANE), F32),
            pltpu.VMEM((512, LANE), F32),
            pltpu.VMEM((512, LANE), F32),
            pltpu.VMEM((3, LANE, LANE), F32),
            pltpu.VMEM((LANE, LANE), F32),
            pltpu.VMEM((COLS, 8, LANE), F32),
            DMA((CHUNKS + 1,)), DMA((CHUNKS + 1,)),
            DMA((CHUNKS,)), DMA((CHUNKS,)),
            DMA((4,)), DMA((4,)),
            DMA((HALO_SEMS,)), DMA((HALO_SEMS,)),
            DMA((2,)), DMA((2,)),
            DMA((6,)), DMA((6,)),
            DMA((COLS,)), DMA((COLS,)),
            DMA((COLS,)), DMA((COLS,)),
        ],
        compiler_params=pltpu.CompilerParams(
            collective_id=2 if last else 1, has_side_effects=True, vmem_limit_bytes=48 * 2**20
        ),
        name="last_update" if last else "update",
    )(acc, ext, pacc, flat, kf, ks)


def body(object_field, probe, positions, amplitudes, live, kernel_first, kernel_second):
    left, right = dft_tables()
    left, right = jnp.asarray(left), jnp.asarray(right)
    base = jnp.stack([lax.axis_index("row") * W, lax.axis_index("col") * W])
    local = positions - base[None, :]
    iters = kernel_first.shape[0]
    ext, flat = halo_call(object_field, probe)
    for step in range(iters):
        acc, pacc = window_call(local, live, ext, flat, amplitudes, left, right)
        ext, flat = update_call(step == iters - 1, acc, ext, pacc, flat, kernel_first[step], kernel_second[step])

    def whole(x):
        return x.reshape(2, 2, W, LANE).transpose(0, 2, 1, 3).reshape(2, W, W)

    return whole(ext), whole(flat)


def solution(mesh):
    return jax.shard_map(
        body,
        mesh=mesh,
        in_specs=(
            P(None, "row", "col"),
            P(),
            P(("row", "col"), None),
            P(("row", "col"), None, None),
            P(("row", "col")),
            P(),
            P(),
        ),
        out_specs=(P(None, "row", "col"), P()),
        check_vma=False,
    )
```

```python
import functools
import math

import jax
import jax.numpy as jnp
import ml_dtypes
import numpy as np
from jax import lax
from jax.experimental import pallas as pl
from jax.experimental.pallas import tpu as pltpu
from jax.sharding import PartitionSpec as P

W = 256
LANE = 128
H = W // 2
G = 2
VLIM = 32 * 2**20
ROWS = 8
COLS = 16
CHUNKS = 4
CH = W // CHUNKS
MESH = pl.DeviceIdType.MESH
F32 = jnp.float32
BF16 = jnp.bfloat16
VM = pl.BlockSpec(memory_space=pltpu.VMEM)
SM = pl.BlockSpec(memory_space=pltpu.SMEM)
ANY = pl.BlockSpec(memory_space=pl.ANY)
EXT = jax.ShapeDtypeStruct((2, 4, 2 * W, LANE), F32)
FLAT = jax.ShapeDtypeStruct((4 * W, LANE), F32)
TILE = jax.ShapeDtypeStruct((2, W, W), F32)
DMA = pltpu.SemaphoreType.DMA


def dft_tables():
    steps = np.arange(W)
    product = (steps[:, None] * steps[None, :]) % W
    angle = product.astype(np.float32) * np.float32(2.0 * math.pi / W)
    scale = np.float32(1.0 / math.sqrt(W))
    fr = (np.cos(angle) * scale).astype(ml_dtypes.bfloat16)
    fi = (-np.sin(angle) * scale).astype(ml_dtypes.bfloat16)
    order = np.concatenate([np.arange(0, W, 2), np.arange(1, W, 2)])
    left = np.block([[fr, -fi], [fi, fr]])[np.concatenate([order, order + W])]
    right = left.T
    right = np.concatenate([right[:, :H], right[:, W : W + H], right[:, H:W], right[:, W + H :]], axis=1)
    halves = []
    for odd in range(2):
        re, im = fr[odd::2, :H], fi[odd::2, :H]
        g = np.block([[re, -im], [im, re]])
        halves += [g, g.T]
    sort = np.zeros((W, W), np.float32)
    sort[np.arange(W), np.argsort(order)] = 1.0
    return np.ascontiguousarray(left), np.ascontiguousarray(right), np.stack(halves), sort.astype(ml_dtypes.bfloat16)


def dot(a, b):
    return jnp.dot(a, b, preferred_element_type=F32)


def window_kernel(pos, live, ext, probe, amps, ltab, rtab, tab, acc, pacc, win, ebuf, abuf, dbuf, bbuf, cbuf):
    slots = amps.shape[0]
    groups = slots // G

    def zero(i, _):
        rows = pl.ds(pl.multiple_of(i * 8, 8), 8)
        for part in range(2):
            for t in range(4):
                acc[part, t, rows, :] = jnp.zeros((8, LANE), F32)
        return 0

    lax.fori_loop(0, 64, zero, 0)

    def zero_probe(i, _):
        pacc[pl.ds(pl.multiple_of(i * 64, 64), 64), :] = jnp.zeros((64, LANE), F32)
        return 0

    lax.fori_loop(0, 16, zero_probe, 0)

    def zero_last(i, _):
        rows = pl.ds(pl.multiple_of(i * 16, 16), 16)
        for g in range(G):
            for part in range(2):
                win[1, g, part, rows, :] = jnp.zeros((16, W), F32)
                cbuf[1, g, part, rows, :] = jnp.zeros((16, W), F32)
        return 0

    lax.fori_loop(0, 16, zero_last, 0)
    B = 16
    lane = lax.broadcasted_iota(jnp.int32, (B, LANE), 1)

    def place_of(s):
        r = jnp.bitwise_and(pos[0, s], W - 1)
        c = jnp.bitwise_and(pos[1, s], W - 1)
        q = c // LANE
        return r, q, c - q * LANE

    def form(s, m, g, i):
        r, q, sh = place_of(s)
        keep = lane < LANE - sh
        o = i * B
        rows = pl.ds(o, B)
        w = []
        for part in range(2):
            cuts = [pltpu.roll(ext[part, q + u, pl.ds(r + o, B), :], LANE - sh, 1) for u in range(3)]
            w.append([jnp.where(keep, cuts[t], cuts[t + 1]) for t in range(2)])
        for t in range(2):
            cols = slice(t * LANE, (t + 1) * LANE)
            w0, w1 = w[0][t], w[1][t]
            win[m, g, 0, rows, cols] = w0
            win[m, g, 1, rows, cols] = w1
            pr = probe[pl.ds(t * W + o, B), :]
            pi = probe[pl.ds((2 + t) * W + o, B), :]
            ebuf[m, g, rows, cols] = (pr * w0 - pi * w1).astype(BF16)
            ebuf[m, g, pl.ds(W + o, B), cols] = (pr * w1 + pi * w0).astype(BF16)

    def left(m, g, half):
        x = dot(ltab[half * W : (half + 1) * W], ebuf[m, g]).astype(BF16)
        abuf[g, :, half * W : (half + 1) * W] = x

    def right(s, g, odd):
        on = s < live[0]
        y = dot(abuf[g], rtab[:, odd * W : (odd + 1) * W])
        for k in range(2):
            rows = slice(k * H, (k + 1) * H)
            yr, yi = y[rows, :H], y[rows, H:]
            amp = amps[s, rows, odd * H : (odd + 1) * H].astype(F32)
            f = amp * lax.rsqrt(jnp.maximum(yr * yr + yi * yi, 0.0625)) - 1.0
            f = jnp.where(on, f, 0.0)
            dbuf[g, k, :H, odd * H : (odd + 1) * H] = (f * yr).astype(BF16)
            dbuf[g, k, H:, odd * H : (odd + 1) * H] = (f * yi).astype(BF16)

    def unleft(g):
        be = dot(tab[1], dbuf[g, 0])
        bo = dot(tab[3], dbuf[g, 1])
        for sign in range(2):
            b = (be - bo if sign else be + bo).astype(BF16)
            rows = slice(sign * H, (sign + 1) * H)
            for odd in range(2):
                cols = slice(odd * H, (odd + 1) * H)
                bbuf[g, odd, rows, :H] = b[:H, cols]
                bbuf[g, odd, rows, H:] = b[H:, cols]

    def unright(m, g, odd):
        cbuf[m, g, odd] = dot(bbuf[g, odd], tab[2 * odd])

    def put(s, m, g, i):
        r, q, sh = place_of(s)
        keep = lane >= sh
        o = i * B
        rows = pl.ds(o, B)
        terms = [[], []]
        er, ei = cbuf[m, g, 0, rows, :H], cbuf[m, g, 0, rows, H:]
        dr, di = cbuf[m, g, 1, rows, :H], cbuf[m, g, 1, rows, H:]
        for t in range(2):
            cols = slice(t * LANE, (t + 1) * LANE)
            at_re = pl.ds(t * W + o, B)
            at_im = pl.ds((2 + t) * W + o, B)
            pr = probe[at_re, :]
            pi = probe[at_im, :]
            cr, ci = (er - dr, ei - di) if t else (er + dr, ei + di)
            wr = win[m, g, 0, rows, cols]
            wi = win[m, g, 1, rows, cols]
            pacc[at_re, :] += wr * cr + wi * ci
            pacc[at_im, :] += wr * ci - wi * cr
            terms[0].append(pltpu.roll(pr * cr + pi * ci, sh, 1))
            terms[1].append(pltpu.roll(pr * ci - pi * cr, sh, 1))
        at = pl.ds(r + o, B)
        for part in range(2):
            a, b = terms[part]
            acc[part, q, at, :] += jnp.where(keep, a, 0.0)
            acc[part, q + 1, at, :] += jnp.where(keep, b, a)
            acc[part, q + 2, at, :] += jnp.where(keep, 0.0, b)

    def stage(p, m):
        before = jnp.maximum(p - 1, 0)
        after = jnp.minimum(p + 1, groups - 1)
        main = []
        for g in range(G):
            main += [lambda g=g, h=h: left(m, g, h) for h in range(2)]
        for g in range(G):
            main += [lambda g=g, h=h: right(p * G + g, g, h) for h in range(2)]
        for g in range(G):
            main += [lambda g=g: unleft(g)]
        for g in range(G):
            main += [lambda g=g, h=h: unright(m, g, h) for h in range(2)]
        side = []
        for g in range(G):
            for i in range(W // B):
                side += [lambda g=g, i=i: put(before * G + g, 1 - m, g, i), lambda g=g, i=i: form(after * G + g, 1 - m, g, i)]
        done = 0
        for n, work in enumerate(main):
            work()
            upto = len(side) * (n + 1) // len(main)
            for extra in side[done:upto]:
                extra()
            done = upto

    for g in range(G):
        for i in range(W // B):
            form(g, 0, g, i)

    def step(p, _):
        stage(2 * p, 0)
        stage(2 * p + 1, 1)
        return 0

    lax.fori_loop(0, groups // 2, step, 0)
    for g in range(G):
        for i in range(W // B):
            put(slots - G + g, 1, g, i)


def window_call(places, live, ext, probe, amps, ltab, rtab, tab):
    return pl.pallas_call(
        window_kernel,
        out_shape=(EXT, FLAT),
        in_specs=[SM, SM, VM, VM, VM, VM, VM, VM],
        out_specs=(VM, VM),
        scratch_shapes=[
            pltpu.VMEM((2, G, 2, W, W), F32),
            pltpu.VMEM((2, G, 2 * W, W), BF16),
            pltpu.VMEM((G, W, 2 * W), BF16),
            pltpu.VMEM((G, 2, W, W), BF16),
            pltpu.VMEM((G, 2, W, W), BF16),
            pltpu.VMEM((2, G, 2, W, W), F32),
        ],
        compiler_params=pltpu.CompilerParams(vmem_limit_bytes=VLIM),
        name="windows",
    )(places, live, ext, probe, amps, ltab, rtab, tab)


def remote(src, dst, send, recv, to):
    return pltpu.make_async_remote_copy(
        src_ref=src, dst_ref=dst, send_sem=send, recv_sem=recv, device_id=to, device_id_type=MESH
    )


def where_am_i():
    row = lax.axis_index("row")
    col = lax.axis_index("col")
    up = (lax.rem(row + ROWS - 1, ROWS), col)
    down = (lax.rem(row + 1, ROWS), col)
    west = (row, lax.rem(col + COLS - 1, COLS))
    east = (row, lax.rem(col + 1, COLS))
    return row, col, up, down, west, east


def greet(targets):
    barrier = pltpu.get_barrier_semaphore()
    for target in targets:
        pl.semaphore_signal(barrier, inc=1, device_id=target, device_id_type=MESH)
    pl.semaphore_wait(barrier, len(targets))


def chunk(k, base=0):
    return pl.ds(base + k * CH, CH)


def halo_copies(tile, ext, send, recv, west, up):
    far = pl.ds(2, 2)
    to_west = [remote(tile(k), ext.at[:, far, chunk(k), :], send.at[k], recv.at[k], west) for k in range(CHUNKS)]
    base = CHUNKS
    to_up = [
        remote(tile(k), ext.at[:, pl.ds(0, 2), chunk(k, W), :], send.at[base + k], recv.at[base + k], up)
        for k in range(CHUNKS)
    ]
    base = 2 * CHUNKS
    onward = [
        remote(
            ext.at[:, far, chunk(k), :], ext.at[:, far, chunk(k, W), :], send.at[base + k], recv.at[base + k], up
        )
        for k in range(CHUNKS)
    ]
    return to_west, to_up, onward


def halo_finish(copies):
    to_west, to_up, onward = copies
    for first, second in zip(to_west, onward):
        first.wait_recv()
        second.start()
    for copy in [*to_up, *onward]:
        copy.wait_recv()
    for copy in [*to_west, *to_up, *onward]:
        copy.wait_send()


HALO_SEMS = 3 * CHUNKS


def halo_kernel(obj, probe, amps, sort, ext, flat, amps_out, amps_in, send, recv, local, amp_sem):
    row, col, up, down, west, east = where_am_i()
    slots = amps.shape[0]
    inward = [
        pltpu.make_async_copy(obj.at[:, :, pl.ds(t * LANE, LANE)], ext.at[:, t, pl.ds(0, W), :], local.at[t])
        for t in range(2)
    ]
    fill = pltpu.make_async_copy(amps, amps_in, amp_sem)
    lay = [
        pltpu.make_async_copy(
            probe.at[part, :, pl.ds(t * LANE, LANE)],
            flat.at[pl.ds((part * 2 + t) * W, W), :],
            local.at[2 + part * 2 + t],
        )
        for part in range(2)
        for t in range(2)
    ]
    for copy in [*inward, fill, *lay]:
        copy.start()
    greet([up, down, west, east])
    inward[0].wait()
    inward[1].wait()
    copies = halo_copies(lambda k: ext.at[:, pl.ds(0, 2), chunk(k), :], ext, send, recv, west, up)
    for copy in copies[0]:
        copy.start()
    for copy in copies[1]:
        copy.start()
    fill.wait()

    def reorder(s, _):
        rows = lax.dot_general(sort[...], amps_in[s], (((0,), (0,)), ((), ())), preferred_element_type=F32)
        amps_out[s] = dot(rows.astype(BF16), sort[...]).astype(BF16)
        return 0

    lax.fori_loop(0, slots, reorder, 0)
    for copy in lay:
        copy.wait()
    halo_finish(copies)


def halo_call(obj, probe, amps, sort):
    return pl.pallas_call(
        halo_kernel,
        out_shape=(EXT, FLAT, jax.ShapeDtypeStruct(amps.shape, BF16)),
        in_specs=[ANY, ANY, ANY, VM],
        out_specs=(VM, VM, VM),
        scratch_shapes=[
            pltpu.VMEM(amps.shape, BF16),
            DMA((HALO_SEMS,)),
            DMA((HALO_SEMS,)),
            DMA((6,)),
            DMA,
        ],
        compiler_params=pltpu.CompilerParams(collective_id=0, has_side_effects=True, vmem_limit_bytes=VLIM),
        name="first_halo",
    )(obj, probe, amps, sort)


TOP = 16
FRAME = W + 2 * TOP


def correlate_block(v, o, kernel, slabs, lane):
    sums = []
    for t in range(3):
        above, here, below = (v(t, o + a) for a in (-1, 0, 1))
        sums.append([above * kernel(0, b) + here * kernel(1, b) + below * kernel(2, b) for b in range(3)])
    before = [pltpu.roll(sums[t][0], 1, 1) for t in range(3)]
    after = [pltpu.roll(sums[t][2], LANE - 1, 1) for t in range(3)]
    return [
        sums[t][1]
        + jnp.where(lane == 0, before[(t + 2) % 3], before[t])
        + jnp.where(lane == LANE - 1, after[(t + 1) % 3], after[t])
        for t in slabs
    ]


def update_kernel(
    step, last, acc, ext_old, pacc, flat_old, kernel_first, kernel_second, ext, flat,
    from_up, from_west, onward, rim_out, rim_in, frame, real,
    p1, h1, p2, h2, p3,
    y_send, y_recv, x_send, x_recv, rim_send, rim_recv, h_send, h_recv,
    a_send, a_recv, b_send, b_recv, c_send, c_recv, d_send, d_recv,
):
    row, col, up, down, west, east = where_am_i()
    core = lax.rem(row, 2)
    y = row // 2
    mate = (row + 1 - 2 * core, col)
    beyond = (lax.rem(row + ROWS - 1 + 2 * core, ROWS), col)
    in_y = [(lax.rem(row + 2 * d, ROWS), col) for d in range(1, 4)]
    in_col = [(row, lax.rem(col + d, COLS)) for d in range(1, COLS)]
    greet([mate, beyond, *in_y, *in_col])

    y_copies = [
        remote(acc.at[:, pl.ds(2, 2), chunk(k, W), :], from_up.at[:, pl.ds(2, 2), chunk(k), :], y_send.at[k], y_recv.at[k], down)
        for k in range(CHUNKS)
    ]
    y_copies.append(
        remote(acc.at[:, pl.ds(0, 2), pl.ds(W, W), :], from_up.at[:, pl.ds(0, 2), :, :], y_send.at[CHUNKS], y_recv.at[CHUNKS], down)
    )
    for copy in y_copies:
        copy.start()

    mine = pl.multiple_of(core * 512, 512)
    other = pl.multiple_of(512 - core * 512, 512)
    a_copies = [remote(pacc.at[pl.ds(other, 512), :], p1, a_send.at[0], a_recv.at[0], mate)]
    a_copies[0].start()

    x_copies = []
    for k in range(CHUNKS):
        y_copies[k].wait_recv()

        def join(i, _):
            o = pl.multiple_of(i * 16, 16)
            for part in range(2):
                for t in range(2):
                    onward[part, t, pl.ds(k * CH + o, 16), :] = (
                        acc[part, 2 + t, pl.ds(k * CH + o, 16), :] + from_up[part, 2 + t, pl.ds(k * CH + o, 16), :]
                    )
            return 0

        lax.fori_loop(0, CH // 16, join, 0)
        copy = remote(onward.at[:, :, chunk(k), :], from_west.at[:, :, chunk(k), :], x_send.at[k], x_recv.at[k], east)
        copy.start()
        x_copies.append(copy)

    a_copies[0].wait_recv()

    def join_half(i, _):
        o = pl.multiple_of(i * 64, 64)
        h1[pl.ds(o, 64), :] = pacc[pl.ds(mine + o, 64), :] + p1[pl.ds(o, 64), :]
        return 0

    lax.fori_loop(0, 8, join_half, 0)
    b_copies = []
    for d in range(1, 4):
        block = pl.multiple_of(lax.rem(y + d, 4) * LANE, LANE)
        b_copies.append(remote(h1.at[pl.ds(block, LANE), :], p2.at[d - 1], b_send.at[d - 1], b_recv.at[d - 1], in_y[d - 1]))
    for copy in b_copies:
        copy.start()

    for t in range(3):
        for part in range(2):
            frame[part, t, pl.ds(0, 8), :] = jnp.zeros((8, LANE), F32)
            frame[part, t, pl.ds(FRAME - 8, 8), :] = jnp.zeros((8, LANE), F32)

    def step_rows(k):
        def add(i, _):
            o = pl.multiple_of(k * CH + i * 16, 16)
            rows = pl.ds(o, 16)
            for part in range(2):
                for t in range(2):
                    total = acc[part, t, rows, :] + from_up[part, t, rows, :] + from_west[part, t, rows, :]
                    frame[part, 1 + t, pl.ds(TOP + o, 16), :] = ext_old[part, t, rows, :] + total * (1.0 / 16.0)
            return 0

        lax.fori_loop(0, CH // 16, add, 0)

    y_copies[CHUNKS].wait_recv()
    for k in range(CHUNKS // 2):
        x_copies[k].wait_recv()
        step_rows(k)

    for copy in b_copies:
        copy.wait_recv()
    here = pl.multiple_of(y * LANE, LANE)
    h2[...] = h1[pl.ds(here, LANE), :] + p2[0] + p2[1] + p2[2]
    c_copies = []
    for d in range(1, COLS):
        block = pl.multiple_of(lax.rem(col + d, COLS) * 8, 8)
        c_copies.append(remote(h2.at[pl.ds(block, 8), :], p3.at[d], c_send.at[d], c_recv.at[d], in_col[d - 1]))
    for copy in c_copies:
        copy.start()

    for k in range(CHUNKS // 2, CHUNKS):
        x_copies[k].wait_recv()
        step_rows(k)

    side = lax.broadcasted_iota(jnp.int32, (W, LANE), 1) < LANE // 2
    for part in range(2):
        ends = jnp.where(side, frame[part, 1, pl.ds(TOP, W), :], frame[part, 2, pl.ds(TOP, W), :]).T
        rim_out[0, part, :, :] = ends[:8, :]
        rim_out[1, part, :, :] = ends[LANE - 8 :, :]
    rims = [
        remote(rim_out.at[0], rim_in.at[0], rim_send.at[0], rim_recv.at[0], west),
        remote(rim_out.at[1], rim_in.at[1], rim_send.at[1], rim_recv.at[1], east),
    ]
    rims[0].start()
    rims[1].start()

    for copy in c_copies:
        copy.wait_recv()
    own = pl.multiple_of(col * 8, 8)
    total = h2[pl.ds(own, 8), :]
    for d in range(1, COLS):
        total = total + p3[d]
    piece = pl.multiple_of(core * 512 + y * LANE + col * 8, 8)
    flat[pl.ds(piece, 8), :] = flat_old[pl.ds(piece, 8), :] + total * (2.0 / math.sqrt(2048.0))
    d_copies = []
    for d in range(1, COLS):
        d_copies.append(
            remote(flat.at[pl.ds(piece, 8), :], flat.at[pl.ds(piece, 8), :], d_send.at[d], d_recv.at[d], in_col[d - 1])
        )
    for copy in d_copies:
        copy.start()

    rims[0].wait_recv()
    rims[1].wait_recv()
    blank = jnp.zeros((LANE - 16, W), F32)
    for part in range(2):
        right_rim = jnp.where(col < COLS - 1, rim_in[0, part, :, :], 0.0)
        left_rim = jnp.where(col > 0, rim_in[1, part, :, :], 0.0)
        frame[part, 0, pl.ds(TOP, W), :] = jnp.concatenate([right_rim, blank, left_rim], axis=0).T
    rows_out = [
        remote(frame.at[:, :, pl.ds(TOP, 8), :], frame.at[:, :, pl.ds(TOP + W, 8), :], rim_send.at[2], rim_recv.at[2], up),
        remote(frame.at[:, :, pl.ds(TOP + W - 8, 8), :], frame.at[:, :, pl.ds(TOP - 8, 8), :], rim_send.at[3], rim_recv.at[3], down),
    ]
    rows_out[0].start()
    rows_out[1].start()

    def gathered(first, count, send, recv, to):
        return remote(flat.at[pl.ds(first, count), :], flat.at[pl.ds(first, count), :], send, recv, to)

    for copy in d_copies:
        copy.wait_recv()
    quarter = pl.multiple_of(core * 512 + y * LANE, LANE)
    for d in range(1, 4):
        b_copies.append(gathered(quarter, LANE, b_send.at[2 + d], b_recv.at[2 + d], in_y[d - 1]))
        b_copies[-1].start()

    rows_out[0].wait_recv()
    rows_out[1].wait_recv()
    for part in range(2):
        for t in range(3):
            top = pl.ds(TOP - 8, 8)
            low = pl.ds(TOP + W, 8)
            frame[part, t, top, :] = jnp.where(row > 0, frame[part, t, top, :], 0.0)
            frame[part, t, low, :] = jnp.where(row < ROWS - 1, frame[part, t, low, :], 0.0)

    lane8 = lax.broadcasted_iota(jnp.int32, (8, LANE), 1)
    lane32 = lax.broadcasted_iota(jnp.int32, (32, LANE), 1)
    west_on = (col > 0).astype(F32)
    east_on = (col < COLS - 1).astype(F32)

    def tap(ref):
        return lambda a, b: ref[a, step, b]

    def first(o, count, lane, keep):
        parts = correlate_block(lambda t, at: frame[1, t, pl.ds(at, count), :], o, tap(kernel_first), range(3), lane)
        for t in range(3):
            value = frame[0, t, pl.ds(o, count), :] + jnp.tanh(parts[t])
            if t == 0:
                value = value * jnp.where(lane < LANE // 2, east_on, west_on)
            if keep is not None:
                value = value * keep
            real[t, pl.ds(o, count), :] = value

    first(TOP - 8, 8, lane8, (row > 0).astype(F32))
    first(TOP + W, 8, lane8, (row < ROWS - 1).astype(F32))

    def first_rows(i, _):
        first(pl.multiple_of(TOP + i * 32, 16), 32, lane32, None)
        return 0

    lax.fori_loop(0, W // 32, first_rows, 0)

    def second(i):
        o = pl.multiple_of(TOP + i * 32, 16)
        at = pl.ds(pl.multiple_of(i * 32, 32), 32)
        parts = correlate_block(lambda t, a: real[t, pl.ds(a, 32), :], o, tap(kernel_second), range(1, 3), lane32)
        for t in range(2):
            new_re = real[1 + t, pl.ds(o, 32), :]
            new_im = frame[1, 1 + t, pl.ds(o, 32), :] + jnp.tanh(parts[t])
            if last:
                ext[0, at, t * LANE : (t + 1) * LANE] = new_re
                ext[1, at, t * LANE : (t + 1) * LANE] = new_im
            else:
                ext[0, t, at, :] = new_re
                ext[1, t, at, :] = new_im

    def second_rows(i, _):
        second(i)
        return 0

    if not last:
        copies = halo_copies(lambda k: ext.at[:, pl.ds(0, 2), chunk(k), :], ext, h_send, h_recv, west, up)
    for k in range(CHUNKS):
        lax.fori_loop(k * CH // 32, (k + 1) * CH // 32, second_rows, 0)
        if not last:
            copies[0][k].start()
            copies[1][k].start()

    for copy in b_copies[3:]:
        copy.wait_recv()
    a_copies.append(gathered(mine, 512, a_send.at[1], a_recv.at[1], mate))
    a_copies[1].start()
    if not last:
        halo_finish(copies)
    a_copies[1].wait_recv()
    for copy in [*y_copies, *x_copies, *a_copies, *b_copies, *c_copies, *d_copies, *rims, *rows_out]:
        copy.wait_send()


def update_call(step, last, acc, ext, pacc, flat, kernel_first, kernel_second):
    return pl.pallas_call(
        functools.partial(update_kernel, step, last),
        out_shape=(TILE if last else EXT, FLAT),
        in_specs=[VM, VM, VM, VM, SM, SM],
        out_specs=(VM, VM),
        scratch_shapes=[
            pltpu.VMEM((2, 4, W, LANE), F32),
            pltpu.VMEM((2, 2, W, LANE), F32),
            pltpu.VMEM((2, 2, W, LANE), F32),
            pltpu.VMEM((2, 2, 8, W), F32),
            pltpu.VMEM((2, 2, 8, W), F32),
            pltpu.VMEM((2, 3, FRAME, LANE), F32),
            pltpu.VMEM((3, FRAME, LANE), F32),
            pltpu.VMEM((512, LANE), F32),
            pltpu.VMEM((512, LANE), F32),
            pltpu.VMEM((3, LANE, LANE), F32),
            pltpu.VMEM((LANE, LANE), F32),
            pltpu.VMEM((COLS, 8, LANE), F32),
            DMA((CHUNKS + 1,)), DMA((CHUNKS + 1,)),
            DMA((CHUNKS,)), DMA((CHUNKS,)),
            DMA((4,)), DMA((4,)),
            DMA((HALO_SEMS,)), DMA((HALO_SEMS,)),
            DMA((2,)), DMA((2,)),
            DMA((6,)), DMA((6,)),
            DMA((COLS,)), DMA((COLS,)),
            DMA((COLS,)), DMA((COLS,)),
        ],
        compiler_params=pltpu.CompilerParams(
            collective_id=2 if last else 1, has_side_effects=True, vmem_limit_bytes=VLIM
        ),
        name="last_update" if last else "update",
    )(acc, ext, pacc, flat, kernel_first, kernel_second)


def body(object_field, probe, positions, amplitudes, live, kernel_first, kernel_second):
    ltab, rtab, tab, sort = (jnp.asarray(table) for table in dft_tables())
    places = positions.T
    kernel_first = kernel_first.transpose(1, 0, 2)
    kernel_second = kernel_second.transpose(1, 0, 2)
    iters = kernel_first.shape[1]
    ext, flat, amps = halo_call(object_field, probe, amplitudes, sort)
    for step in range(iters):
        acc, pacc = window_call(places, live, ext, flat, amps, ltab, rtab, tab)
        ext, flat = update_call(step, step == iters - 1, acc, ext, pacc, flat, kernel_first, kernel_second)
    return ext, flat.reshape(2, 2, W, LANE).transpose(0, 2, 1, 3).reshape(2, W, W)


def solution(mesh):
    return jax.shard_map(
        body,
        mesh=mesh,
        in_specs=(
            P(None, "row", "col"),
            P(),
            P(("row", "col"), None),
            P(("row", "col"), None, None),
            P(("row", "col")),
            P(),
            P(),
        ),
        out_specs=(P(None, "row", "col"), P()),
        check_vma=False,
    )
```

```python
import functools
import math

import jax
import jax.numpy as jnp
import ml_dtypes
import numpy as np
from jax import lax
from jax.experimental import pallas as pl
from jax.experimental.pallas import tpu as pltpu
from jax.sharding import PartitionSpec as P

W = 256
LANE = 128
H = W // 2
G = 2
VLIM = 32 * 2**20
ROWS = 8
COLS = 16
SPILL = (8, 96, 176, 224, 248)
FIRST = (0, 32, 64, 96, 128, 160, 192, 224, 256)
REAL = (0, 80, 160, 208, 256)
LATER = (0, 64, 128, 192, 256)
MESH = pl.DeviceIdType.MESH
F32 = jnp.float32
BF16 = jnp.bfloat16
VM = pl.BlockSpec(memory_space=pltpu.VMEM)
SM = pl.BlockSpec(memory_space=pltpu.SMEM)
ANY = pl.BlockSpec(memory_space=pl.ANY)
EXT = jax.ShapeDtypeStruct((2, 4, 2 * W, LANE), F32)
FLAT = jax.ShapeDtypeStruct((4 * W, LANE), F32)
TILE = jax.ShapeDtypeStruct((2, W, W), F32)
DMA = pltpu.SemaphoreType.DMA


def dft_tables():
    steps = np.arange(W)
    product = (steps[:, None] * steps[None, :]) % W
    angle = product.astype(np.float32) * np.float32(2.0 * math.pi / W)
    scale = np.float32(1.0 / math.sqrt(W))
    fr = (np.cos(angle) * scale).astype(ml_dtypes.bfloat16)
    fi = (-np.sin(angle) * scale).astype(ml_dtypes.bfloat16)
    order = np.concatenate([np.arange(0, W, 2), np.arange(1, W, 2)])
    left = np.block([[fr, -fi], [fi, fr]])[np.concatenate([order, order + W])]
    right = left.T
    right = np.concatenate([right[:, :H], right[:, W : W + H], right[:, H:W], right[:, W + H :]], axis=1)
    halves = []
    for odd in range(2):
        re, im = fr[odd::2, :H], fi[odd::2, :H]
        g = np.block([[re, -im], [im, re]])
        halves += [g, g.T]
    sort = np.zeros((W, W), np.float32)
    sort[np.arange(W), np.argsort(order)] = 1.0
    return np.ascontiguousarray(left), np.ascontiguousarray(right), np.stack(halves), sort.astype(ml_dtypes.bfloat16)


def dot(a, b):
    return jnp.dot(a, b, preferred_element_type=F32)


def window_kernel(pos, live, ext, probe, amps, ltab, rtab, tab, acc, pacc, win, ebuf, abuf, dbuf, bbuf, cbuf):
    slots = amps.shape[0]
    groups = slots // G

    def zero(i, _):
        rows = pl.ds(pl.multiple_of(i * 8, 8), 8)
        for part in range(2):
            for t in range(4):
                acc[part, t, rows, :] = jnp.zeros((8, LANE), F32)
        return 0

    lax.fori_loop(0, 64, zero, 0)

    def zero_probe(i, _):
        pacc[pl.ds(pl.multiple_of(i * 64, 64), 64), :] = jnp.zeros((64, LANE), F32)
        return 0

    lax.fori_loop(0, 16, zero_probe, 0)

    def zero_last(i, _):
        rows = pl.ds(pl.multiple_of(i * 16, 16), 16)
        for g in range(G):
            for part in range(2):
                win[1, g, part, rows, :] = jnp.zeros((16, W), F32)
                cbuf[1, g, part, rows, :] = jnp.zeros((16, W), F32)
        return 0

    lax.fori_loop(0, 16, zero_last, 0)
    B = 16
    lane = lax.broadcasted_iota(jnp.int32, (B, LANE), 1)

    def place_of(s):
        r = jnp.bitwise_and(pos[0, s], W - 1)
        c = jnp.bitwise_and(pos[1, s], W - 1)
        q = c // LANE
        return r, q, c - q * LANE

    def form(s, m, g, i):
        r, q, sh = place_of(s)
        keep = lane < LANE - sh
        o = i * B
        rows = pl.ds(o, B)
        w = []
        for part in range(2):
            cuts = [pltpu.roll(ext[part, q + u, pl.ds(r + o, B), :], LANE - sh, 1) for u in range(3)]
            w.append([jnp.where(keep, cuts[t], cuts[t + 1]) for t in range(2)])
        for t in range(2):
            cols = slice(t * LANE, (t + 1) * LANE)
            w0, w1 = w[0][t], w[1][t]
            win[m, g, 0, rows, cols] = w0
            win[m, g, 1, rows, cols] = w1
            pr = probe[pl.ds(t * W + o, B), :]
            pi = probe[pl.ds((2 + t) * W + o, B), :]
            ebuf[m, g, rows, cols] = (pr * w0 - pi * w1).astype(BF16)
            ebuf[m, g, pl.ds(W + o, B), cols] = (pr * w1 + pi * w0).astype(BF16)

    def left(m, g, half):
        x = dot(ltab[half * W : (half + 1) * W], ebuf[m, g]).astype(BF16)
        abuf[g, :, half * W : (half + 1) * W] = x

    def right(s, g, odd):
        on = s < live[0]
        y = dot(abuf[g], rtab[:, odd * W : (odd + 1) * W])
        for k in range(2):
            rows = slice(k * H, (k + 1) * H)
            yr, yi = y[rows, :H], y[rows, H:]
            amp = amps[s, rows, odd * H : (odd + 1) * H].astype(F32)
            f = amp * lax.rsqrt(jnp.maximum(yr * yr + yi * yi, 0.0625)) - 1.0
            f = jnp.where(on, f, 0.0)
            dbuf[g, k, :H, odd * H : (odd + 1) * H] = (f * yr).astype(BF16)
            dbuf[g, k, H:, odd * H : (odd + 1) * H] = (f * yi).astype(BF16)

    def unleft(g):
        be = dot(tab[1], dbuf[g, 0])
        bo = dot(tab[3], dbuf[g, 1])
        for sign in range(2):
            b = (be - bo if sign else be + bo).astype(BF16)
            rows = slice(sign * H, (sign + 1) * H)
            for odd in range(2):
                cols = slice(odd * H, (odd + 1) * H)
                bbuf[g, odd, rows, :H] = b[:H, cols]
                bbuf[g, odd, rows, H:] = b[H:, cols]

    def unright(m, g, odd):
        cbuf[m, g, odd] = dot(bbuf[g, odd], tab[2 * odd])

    def put(s, m, g, i):
        r, q, sh = place_of(s)
        keep = lane >= sh
        o = i * B
        rows = pl.ds(o, B)
        terms = [[], []]
        er, ei = cbuf[m, g, 0, rows, :H], cbuf[m, g, 0, rows, H:]
        dr, di = cbuf[m, g, 1, rows, :H], cbuf[m, g, 1, rows, H:]
        for t in range(2):
            cols = slice(t * LANE, (t + 1) * LANE)
            at_re = pl.ds(t * W + o, B)
            at_im = pl.ds((2 + t) * W + o, B)
            pr = probe[at_re, :]
            pi = probe[at_im, :]
            cr, ci = (er - dr, ei - di) if t else (er + dr, ei + di)
            wr = win[m, g, 0, rows, cols]
            wi = win[m, g, 1, rows, cols]
            pacc[at_re, :] += wr * cr + wi * ci
            pacc[at_im, :] += wr * ci - wi * cr
            terms[0].append(pltpu.roll(pr * cr + pi * ci, sh, 1))
            terms[1].append(pltpu.roll(pr * ci - pi * cr, sh, 1))
        at = pl.ds(r + o, B)
        for part in range(2):
            a, b = terms[part]
            acc[part, q, at, :] += jnp.where(keep, a, 0.0)
            acc[part, q + 1, at, :] += jnp.where(keep, b, a)
            acc[part, q + 2, at, :] += jnp.where(keep, 0.0, b)

    def stage(p, m):
        before = jnp.maximum(p - 1, 0)
        after = jnp.minimum(p + 1, groups - 1)
        main = []
        for g in range(G):
            main += [lambda g=g, h=h: left(m, g, h) for h in range(2)]
        for g in range(G):
            main += [lambda g=g, h=h: right(p * G + g, g, h) for h in range(2)]
        for g in range(G):
            main += [lambda g=g: unleft(g)]
        for g in range(G):
            main += [lambda g=g, h=h: unright(m, g, h) for h in range(2)]
        side = []
        for g in range(G):
            for i in range(W // B):
                side += [lambda g=g, i=i: put(before * G + g, 1 - m, g, i), lambda g=g, i=i: form(after * G + g, 1 - m, g, i)]
        done = 0
        for n, work in enumerate(main):
            work()
            upto = len(side) * (n + 1) // len(main)
            for extra in side[done:upto]:
                extra()
            done = upto

    for g in range(G):
        for i in range(W // B):
            form(g, 0, g, i)

    def step(p, _):
        stage(2 * p, 0)
        stage(2 * p + 1, 1)
        return 0

    lax.fori_loop(0, groups // 2, step, 0)
    for g in range(G):
        for i in range(W // B):
            put(slots - G + g, 1, g, i)


def window_call(places, live, ext, probe, amps, ltab, rtab, tab):
    return pl.pallas_call(
        window_kernel,
        out_shape=(EXT, FLAT),
        in_specs=[SM, SM, VM, VM, VM, VM, VM, VM],
        out_specs=(VM, VM),
        scratch_shapes=[
            pltpu.VMEM((2, G, 2, W, W), F32),
            pltpu.VMEM((2, G, 2 * W, W), BF16),
            pltpu.VMEM((G, W, 2 * W), BF16),
            pltpu.VMEM((G, 2, W, W), BF16),
            pltpu.VMEM((G, 2, W, W), BF16),
            pltpu.VMEM((2, G, 2, W, W), F32),
        ],
        compiler_params=pltpu.CompilerParams(vmem_limit_bytes=VLIM),
        name="windows",
    )(places, live, ext, probe, amps, ltab, rtab, tab)


def remote(src, dst, send, recv, to):
    return pltpu.make_async_remote_copy(
        src_ref=src, dst_ref=dst, send_sem=send, recv_sem=recv, device_id=to, device_id_type=MESH
    )


def where_am_i():
    row = lax.axis_index("row")
    col = lax.axis_index("col")
    up = (lax.rem(row + ROWS - 1, ROWS), col)
    down = (lax.rem(row + 1, ROWS), col)
    west = (row, lax.rem(col + COLS - 1, COLS))
    east = (row, lax.rem(col + 1, COLS))
    return row, col, up, down, west, east


def greet(targets):
    barrier = pltpu.get_barrier_semaphore()
    for target in targets:
        pl.semaphore_signal(barrier, inc=1, device_id=target, device_id_type=MESH)
    pl.semaphore_wait(barrier, len(targets))


def pieces(bounds, base=0):
    return [pl.ds(base + first, end - first) for first, end in zip(bounds, bounds[1:])]


class Copy:
    def __init__(self, made):
        self.made, self.left = made, False
        self.start, self.wait_recv = made.start, made.wait_recv

    def wait_send(self):
        if not self.left:
            self.left = True
            self.made.wait_send()


class Links:
    def __init__(self, send, recv):
        self.send, self.recv, self.copies = send, recv, []

    def copy(self, src, dst, to):
        at = len(self.copies)
        self.copies.append(Copy(remote(src, dst, self.send.at[at], self.recv.at[at], to)))
        return self.copies[-1]

    def start(self, src, dst, to):
        made = self.copy(src, dst, to)
        made.start()
        return made

    def drain(self):
        for made in self.copies:
            made.wait_send()


def halo_copies(links, ext, bounds, west, up):
    near, far = pl.ds(0, 2), pl.ds(2, 2)
    high, low = pieces(bounds), pieces(bounds, W)
    to_west = [links.copy(ext.at[:, near, a, :], ext.at[:, far, a, :], west) for a in high]
    to_up = [links.copy(ext.at[:, near, a, :], ext.at[:, near, b, :], up) for a, b in zip(high, low)]
    onward = [links.copy(ext.at[:, far, a, :], ext.at[:, far, b, :], up) for a, b in zip(high, low)]
    return to_west, to_up, onward


HALO_SEMS = 3 * (len(FIRST) - 1)
UPDATE_SEMS = 96


def halo_kernel(obj, probe, amps, sort, ext, flat, amps_out, amps_in, send, recv, local, amp_sem):
    row, col, up, down, west, east = where_am_i()
    slots = amps.shape[0]
    inward = [
        pltpu.make_async_copy(obj.at[:, :, pl.ds(t * LANE, LANE)], ext.at[:, t, pl.ds(0, W), :], local.at[t])
        for t in range(2)
    ]
    fill = pltpu.make_async_copy(amps, amps_in, amp_sem)
    lay = [
        pltpu.make_async_copy(
            probe.at[part, :, pl.ds(t * LANE, LANE)],
            flat.at[pl.ds((part * 2 + t) * W, W), :],
            local.at[2 + part * 2 + t],
        )
        for part in range(2)
        for t in range(2)
    ]
    for copy in [*inward, fill, *lay]:
        copy.start()
    greet([up, down, west, east])
    inward[0].wait()
    inward[1].wait()
    links = Links(send, recv)
    copies = halo_copies(links, ext, FIRST, west, up)
    to_west, to_up, onward = copies
    ahead = 4
    for k in range(ahead):
        to_west[k].start()
    to_up[0].start()
    to_up[1].start()
    fill.wait()

    def reorder(s):
        rows = lax.dot_general(sort[...], amps_in[s], (((0,), (0,)), ((), ())), preferred_element_type=F32)
        amps_out[s] = dot(rows.astype(BF16), sort[...]).astype(BF16)

    def reorder_some(first, last):
        def one(s, _):
            reorder(s)
            return 0

        lax.fori_loop(first, last, one, 0)

    count = len(to_west)
    for k in range(count):
        reorder_some(k * slots // count, (k + 1) * slots // count)
        to_west[k].wait_recv()
        onward[k].start()
        if k + ahead < count:
            to_west[k + ahead].start()
        if k + 2 < count:
            to_up[k + 2].start()
    for copy in [*to_up, *onward]:
        copy.wait_recv()
    for copy in lay:
        copy.wait()
    links.drain()


def halo_call(obj, probe, amps, sort):
    return pl.pallas_call(
        halo_kernel,
        out_shape=(EXT, FLAT, jax.ShapeDtypeStruct(amps.shape, BF16)),
        in_specs=[ANY, ANY, ANY, VM],
        out_specs=(VM, VM, VM),
        scratch_shapes=[
            pltpu.VMEM(amps.shape, BF16),
            DMA((HALO_SEMS,)),
            DMA((HALO_SEMS,)),
            DMA((6,)),
            DMA,
        ],
        compiler_params=pltpu.CompilerParams(collective_id=0, has_side_effects=True, vmem_limit_bytes=VLIM),
        name="first_halo",
    )(obj, probe, amps, sort)


TOP = 16
FRAME = W + 2 * TOP


def correlate_block(v, o, kernel, slabs, lane):
    sums = []
    for t in range(3):
        above, here, below = (v(t, o + a) for a in (-1, 0, 1))
        sums.append([above * kernel(0, b) + here * kernel(1, b) + below * kernel(2, b) for b in range(3)])
    before = [pltpu.roll(sums[t][0], 1, 1) for t in range(3)]
    after = [pltpu.roll(sums[t][2], LANE - 1, 1) for t in range(3)]
    return [
        sums[t][1]
        + jnp.where(lane == 0, before[(t + 2) % 3], before[t])
        + jnp.where(lane == LANE - 1, after[(t + 1) % 3], after[t])
        for t in slabs
    ]


def update_kernel(
    step, last, acc, ext_old, pacc, flat_old, kernel_first, kernel_second, ext, flat,
    from_up, from_west, onward, strip, strip_up, strip_west, strip_on, strip_new, rim_in, corner_in, frame, real,
    p1, h1, p2, h3, p4, send, recv,
):
    row, col, up, down, west, east = where_am_i()
    core = lax.rem(row, 2)
    y = row // 2
    mate = (row + 1 - 2 * core, col)
    beyond = (lax.rem(row + ROWS - 1 + 2 * core, ROWS), col)
    in_y = [(lax.rem(row + 2 * d, ROWS), col) for d in range(1, 4)]
    in_col = [(row, lax.rem(col + d, COLS)) for d in range(1, COLS)]
    corners = [(r[0], c[1]) for r in (up, down) for c in (west, east)]
    links = Links(send, recv)
    near, far = pl.ds(0, 2), pl.ds(2, 2)
    ends = (pl.ds(0, 8), pl.ds(W - 8, 8))
    side = lax.broadcasted_iota(jnp.int32, (W, LANE), 1) < LANE // 2

    def sides_of(left, right):
        turned = jnp.where(side, left, right).T
        return jnp.concatenate([turned[:8, :], turned[LANE - 8 :, :]], axis=0)

    def acc_sides(low):
        rows = pl.ds(low * W, W)
        for part in range(2):
            for half in range(2):
                strip[low, part, half, :, :] = sides_of(acc[part, 2 * half, rows, :], acc[part, 2 * half + 1, rows, :])

    acc_sides(1)
    greet([mate, beyond, *in_y, *in_col, *corners])

    first_y = [links.start(strip.at[1], strip_up, down)]
    for a, b in zip(ends, (pl.ds(W, 8), pl.ds(2 * W - 8, 8))):
        first_y.append(links.start(acc.at[:, :, b, :], from_up.at[:, :, a, :], down))
    mine = pl.multiple_of(core * 512, 512)
    other = pl.multiple_of(512 - core * 512, 512)
    halves = links.start(pacc.at[pl.ds(other, 512), :], p1, mate)
    high, low = pieces(SPILL), pieces(SPILL, W)
    y_far = [links.copy(acc.at[:, far, b, :], from_up.at[:, far, a, :], down) for a, b in zip(high, low)]
    y_near = [links.copy(acc.at[:, near, b, :], from_up.at[:, near, a, :], down) for a, b in zip(high, low)]
    y_far[0].start()
    acc_sides(0)
    old_sides = [sides_of(ext_old[part, 0, pl.ds(0, W), :], ext_old[part, 1, pl.ds(0, W), :]) for part in range(2)]

    def join(rows):
        for part in range(2):
            for t in range(2):
                onward[part, t, rows, :] = acc[part, 2 + t, rows, :] + from_up[part, 2 + t, rows, :]

    def step_rows(rows, to):
        for part in range(2):
            for t in range(2):
                total = acc[part, t, rows, :] + from_up[part, t, rows, :] + from_west[part, t, rows, :]
                frame[part, 1 + t, to, :] = ext_old[part, t, rows, :] + total * (1.0 / 16.0)

    def over(bounds, k, size, work):
        def one(i, _):
            work(pl.multiple_of(i * size, size))
            return 0

        lax.fori_loop(bounds[k] // size, bounds[k + 1] // size, one, 0)

    x_copies = []

    def pass_on(k):
        y_far[k].wait_recv()
        over(SPILL, k, 8, lambda o: join(pl.ds(o, 8)))
        rows = pieces(SPILL)[k]
        x_copies.append(links.start(onward.at[:, :, rows, :], from_west.at[:, :, rows, :], east))

    y_far[0].wait_send()
    y_far[1].start()
    halves.wait_recv()

    def join_half(i, _):
        o = pl.multiple_of(i * 64, 64)
        h1[pl.ds(o, 64), :] = pacc[pl.ds(mine + o, 64), :] + p1[pl.ds(o, 64), :]
        return 0

    lax.fori_loop(0, 8, join_half, 0)
    for copy in first_y:
        copy.wait_recv()
    for a in ends:
        join(a)
    for part in range(2):
        strip_on[part, :, :] = strip[0, part, 1, :, :] + strip_up[part, 1, :, :]
    first_x = [links.start(strip_on, strip_west, east)]
    for a in ends:
        first_x.append(links.start(onward.at[:, :, a, :], from_west.at[:, :, a, :], east))

    over_col = []
    for d in range(1, COLS):
        block = pl.multiple_of(lax.rem(col + d, COLS) * 32, 32)
        over_col.append(links.start(h1.at[pl.ds(block, 32), :], p2.at[d - 1], in_col[d - 1]))
    y_far[1].wait_send()
    y_far[2].start()
    y_near[0].start()
    pass_on(0)

    for copy in first_x:
        copy.wait_recv()
    for part in range(2):
        total = strip[0, part, 0, :, :] + strip_up[part, 0, :, :] + strip_west[part, :, :]
        strip_new[part, :, :] = old_sides[part] + total * (1.0 / 16.0)
    step_rows(ends[0], pl.ds(TOP, 8))
    step_rows(ends[1], pl.ds(TOP + W - 8, 8))
    top_in, top_out = pl.ds(TOP - 8, 8), pl.ds(TOP, 8)
    low_in, low_out = pl.ds(TOP + W, 8), pl.ds(TOP + W - 8, 8)
    both = pl.ds(1, 2)
    rims = [
        links.start(strip_new.at[:, pl.ds(0, 8), :], rim_in.at[0], west),
        links.start(strip_new.at[:, pl.ds(8, 8), :], rim_in.at[1], east),
        links.start(frame.at[:, both, top_out, :], frame.at[:, both, low_in, :], up),
        links.start(frame.at[:, both, low_out, :], frame.at[:, both, top_in, :], down),
        links.start(frame.at[:, 1, top_out, :], corner_in.at[0], corners[0]),
        links.start(frame.at[:, 2, top_out, :], corner_in.at[1], corners[1]),
        links.start(frame.at[:, 1, low_out, :], corner_in.at[2], corners[2]),
        links.start(frame.at[:, 2, low_out, :], corner_in.at[3], corners[3]),
    ]
    y_far[2].wait_send()
    y_far[3].start()
    y_near[1].start()
    pass_on(1)
    pass_on(2)
    y_near[2].start()
    for copy in over_col:
        copy.wait_recv()
    here = pl.multiple_of(col * 32, 32)
    total = h1[pl.ds(here, 32), :]
    for d in range(COLS - 1):
        total = total + p2[d]
    h3[...] = total
    over_y = [links.start(h3, p4.at[y], to) for to in in_y]
    p4[y] = total

    for copy in rims:
        copy.wait_recv()
    blank = jnp.zeros((LANE - 16, W), F32)
    lane8 = lax.broadcasted_iota(jnp.int32, (8, LANE), 1)
    for part in range(2):
        right_rim = jnp.where(col < COLS - 1, rim_in[0, part, :, :], 0.0)
        left_rim = jnp.where(col > 0, rim_in[1, part, :, :], 0.0)
        frame[part, 0, pl.ds(TOP, W), :] = jnp.concatenate([right_rim, blank, left_rim], axis=0).T
        for on, rows, right, left in ((row > 0, top_in, 2, 3), (row < ROWS - 1, low_in, 0, 1)):
            right_end = jnp.where(col < COLS - 1, corner_in[right, part, :, :], 0.0)
            left_end = jnp.where(col > 0, corner_in[left, part, :, :], 0.0)
            ends_in = jnp.where(lane8 < 8, right_end, jnp.where(lane8 >= LANE - 8, left_end, 0.0))
            frame[part, 0, rows, :] = jnp.where(on, ends_in, 0.0)
            for t in range(1, 3):
                frame[part, t, rows, :] = jnp.where(on, frame[part, t, rows, :], 0.0)
        for t in range(3):
            frame[part, t, pl.ds(0, 8), :] = jnp.zeros((8, LANE), F32)
            frame[part, t, pl.ds(FRAME - 8, 8), :] = jnp.zeros((8, LANE), F32)

    west_on = (col > 0).astype(F32)
    east_on = (col < COLS - 1).astype(F32)
    lane16 = lax.broadcasted_iota(jnp.int32, (16, LANE), 1)
    lane32 = lax.broadcasted_iota(jnp.int32, (32, LANE), 1)

    def tap(ref):
        return lambda a, b: ref[a, step, b]

    def first(o, count, lane, keep):
        parts = correlate_block(lambda t, at: frame[1, t, pl.ds(at, count), :], o, tap(kernel_first), range(3), lane)
        for t in range(3):
            value = frame[0, t, pl.ds(o, count), :] + jnp.tanh(parts[t])
            if t == 0:
                value = value * jnp.where(lane < LANE // 2, east_on, west_on)
            if keep is not None:
                value = value * keep
            real[t, pl.ds(o, count), :] = value

    first(TOP - 8, 8, lane8, (row > 0).astype(F32))
    first(TOP + W, 8, lane8, (row < ROWS - 1).astype(F32))

    def second(o):
        at = pl.ds(o, 32)
        o = o + TOP
        parts = correlate_block(lambda t, a: real[t, pl.ds(a, 32), :], o, tap(kernel_second), range(1, 3), lane32)
        for t in range(2):
            new_re = real[1 + t, pl.ds(o, 32), :]
            new_im = frame[1, 1 + t, pl.ds(o, 32), :] + jnp.tanh(parts[t])
            if last:
                ext[0, at, t * LANE : (t + 1) * LANE] = new_re
                ext[1, at, t * LANE : (t + 1) * LANE] = new_im
            else:
                ext[0, t, at, :] = new_re
                ext[1, t, at, :] = new_im

    if not last:
        copies = halo_copies(links, ext, LATER, west, up)

    def settle(k):
        y_near[k].wait_recv()
        x_copies[k].wait_recv()
        over(SPILL, k, 8, lambda o: step_rows(pl.ds(o, 8), pl.ds(o + TOP, 8)))
        over(REAL, k, 16, lambda o: first(o + TOP, 16, lane16, None))
        over(LATER, k, 32, second)
        if not last:
            copies[0][k].start()
            copies[1][k].start()

    for copy in over_y:
        copy.wait_recv()
    piece = pl.multiple_of(core * 512 + col * 32, 32)
    total = p4[0] + p4[1] + p4[2] + p4[3]
    flat[pl.ds(piece, 32), :] = flat_old[pl.ds(piece, 32), :] + total * (2.0 / math.sqrt(2048.0))

    def gather(first, count, targets):
        rows = pl.ds(first, count)
        return [links.start(flat.at[rows, :], flat.at[rows, :], to) for to in targets]

    back = gather(piece, 32, in_col)

    settle(0)
    pass_on(3)
    y_near[3].start()
    settle(1)
    settle(2)
    settle(3)
    for copy in back:
        copy.wait_recv()
    back = gather(mine, 512, [mate])
    if not last:
        for k in range(0, 2):
            copies[0][k].wait_recv()
            copies[2][k].start()
    if not last:
        for k in range(2, 4):
            copies[0][k].wait_recv()
            copies[2][k].start()
    if not last:
        for copy in [*copies[1], *copies[2]]:
            copy.wait_recv()
    back[0].wait_recv()
    links.drain()


def update_call(step, last, acc, ext, pacc, flat, kernel_first, kernel_second):
    return pl.pallas_call(
        functools.partial(update_kernel, step, last),
        out_shape=(TILE if last else EXT, FLAT),
        in_specs=[VM, VM, VM, VM, SM, SM],
        out_specs=(VM, VM),
        scratch_shapes=[
            pltpu.VMEM((2, 4, W, LANE), F32),
            pltpu.VMEM((2, 2, W, LANE), F32),
            pltpu.VMEM((2, 2, W, LANE), F32),
            pltpu.VMEM((2, 2, 2, 16, W), F32),
            pltpu.VMEM((2, 2, 16, W), F32),
            pltpu.VMEM((2, 16, W), F32),
            pltpu.VMEM((2, 16, W), F32),
            pltpu.VMEM((2, 16, W), F32),
            pltpu.VMEM((2, 2, 8, W), F32),
            pltpu.VMEM((4, 2, 8, LANE), F32),
            pltpu.VMEM((2, 3, FRAME, LANE), F32),
            pltpu.VMEM((3, FRAME, LANE), F32),
            pltpu.VMEM((512, LANE), F32),
            pltpu.VMEM((512, LANE), F32),
            pltpu.VMEM((COLS - 1, 32, LANE), F32),
            pltpu.VMEM((32, LANE), F32),
            pltpu.VMEM((4, 32, LANE), F32),
            DMA((UPDATE_SEMS,)),
            DMA((UPDATE_SEMS,)),
        ],
        compiler_params=pltpu.CompilerParams(
            collective_id=2 if last else 1, has_side_effects=True, vmem_limit_bytes=VLIM
        ),
        name="last_update" if last else "update",
    )(acc, ext, pacc, flat, kernel_first, kernel_second)


def body(object_field, probe, positions, amplitudes, live, kernel_first, kernel_second):
    ltab, rtab, tab, sort = (jnp.asarray(table) for table in dft_tables())
    places = positions.T
    kernel_first = kernel_first.transpose(1, 0, 2)
    kernel_second = kernel_second.transpose(1, 0, 2)
    iters = kernel_first.shape[1]
    ext, flat, amps = halo_call(object_field, probe, amplitudes, sort)
    for step in range(iters):
        acc, pacc = window_call(places, live, ext, flat, amps, ltab, rtab, tab)
        ext, flat = update_call(step, step == iters - 1, acc, ext, pacc, flat, kernel_first, kernel_second)
    return ext, flat.reshape(2, 2, W, LANE).transpose(0, 2, 1, 3).reshape(2, W, W)


def solution(mesh):
    return jax.shard_map(
        body,
        mesh=mesh,
        in_specs=(
            P(None, "row", "col"),
            P(),
            P(("row", "col"), None),
            P(("row", "col"), None, None),
            P(("row", "col")),
            P(),
            P(),
        ),
        out_specs=(P(None, "row", "col"), P()),
        check_vma=False,
    )
```

```python
import functools
import math

import jax
import jax.numpy as jnp
import ml_dtypes
import numpy as np
from jax import lax
from jax.experimental import pallas as pl
from jax.experimental.pallas import tpu as pltpu
from jax.sharding import PartitionSpec as P

W = 256
LANE = 128
H = W // 2
G = 2
VLIM = 32 * 2**20
ROWS = 8
COLS = 16
SPILL = (8, 96, 176, 224, 248)
FIRST = (0, 32, 64, 96, 128, 160, 192, 224, 256)
REAL = (0, 80, 160, 208, 256)
LATER = (0, 64, 128, 192, 256)
MESH = pl.DeviceIdType.MESH
F32 = jnp.float32
BF16 = jnp.bfloat16
VM = pl.BlockSpec(memory_space=pltpu.VMEM)
SM = pl.BlockSpec(memory_space=pltpu.SMEM)
HBM = pl.BlockSpec(memory_space=pltpu.HBM)
EXT = jax.ShapeDtypeStruct((2, 4, 2 * W, LANE), F32)
FLAT = jax.ShapeDtypeStruct((4 * W, LANE), F32)
TILE = jax.ShapeDtypeStruct((2, W, W), F32)
DMA = pltpu.SemaphoreType.DMA


def dft_tables():
    steps = np.arange(W)
    product = (steps[:, None] * steps[None, :]) % W
    angle = product.astype(np.float32) * np.float32(2.0 * math.pi / W)
    scale = np.float32(1.0 / math.sqrt(W))
    fr = (np.cos(angle) * scale).astype(ml_dtypes.bfloat16)
    fi = (-np.sin(angle) * scale).astype(ml_dtypes.bfloat16)
    order = np.concatenate([np.arange(0, W, 2), np.arange(1, W, 2)])
    left = np.block([[fr, -fi], [fi, fr]])[np.concatenate([order, order + W])]
    right = left.T
    right = np.concatenate([right[:, :H], right[:, W : W + H], right[:, H:W], right[:, W + H :]], axis=1)
    halves = []
    for odd in range(2):
        re, im = fr[odd::2, :H], fi[odd::2, :H]
        g = np.block([[re, -im], [im, re]])
        halves += [g, g.T]
    return np.ascontiguousarray(left), np.ascontiguousarray(right), np.stack(halves)


def dot(a, b):
    return jnp.dot(a, b, preferred_element_type=F32)


def window_kernel(pos, live, ext, probe, amps, ltab, rtab, tab, acc, pacc, win, ebuf, abuf, dbuf, bbuf, cbuf):
    slots = amps.shape[0]
    groups = slots // G

    def zero(i, _):
        rows = pl.ds(pl.multiple_of(i * 8, 8), 8)
        for part in range(2):
            for t in range(4):
                acc[part, t, rows, :] = jnp.zeros((8, LANE), F32)
        return 0

    lax.fori_loop(0, 64, zero, 0)

    def zero_probe(i, _):
        pacc[pl.ds(pl.multiple_of(i * 64, 64), 64), :] = jnp.zeros((64, LANE), F32)
        return 0

    lax.fori_loop(0, 16, zero_probe, 0)

    def zero_last(i, _):
        rows = pl.ds(pl.multiple_of(i * 16, 16), 16)
        for g in range(G):
            for part in range(2):
                win[1, g, part, rows, :] = jnp.zeros((16, W), F32)
                cbuf[1, g, part, rows, :] = jnp.zeros((16, W), F32)
        return 0

    lax.fori_loop(0, 16, zero_last, 0)
    B = 16
    lane = lax.broadcasted_iota(jnp.int32, (B, LANE), 1)

    def place_of(s):
        r = jnp.bitwise_and(pos[0, s], W - 1)
        c = jnp.bitwise_and(pos[1, s], W - 1)
        q = c // LANE
        return r, q, c - q * LANE

    def form(s, m, g, i):
        r, q, sh = place_of(s)
        keep = lane < LANE - sh
        o = i * B
        rows = pl.ds(o, B)
        w = []
        for part in range(2):
            cuts = [pltpu.roll(ext[part, q + u, pl.ds(r + o, B), :], LANE - sh, 1) for u in range(3)]
            w.append([jnp.where(keep, cuts[t], cuts[t + 1]) for t in range(2)])
        for t in range(2):
            cols = slice(t * LANE, (t + 1) * LANE)
            w0, w1 = w[0][t], w[1][t]
            win[m, g, 0, rows, cols] = w0
            win[m, g, 1, rows, cols] = w1
            pr = probe[pl.ds(t * W + o, B), :]
            pi = probe[pl.ds((2 + t) * W + o, B), :]
            ebuf[m, g, rows, cols] = (pr * w0 - pi * w1).astype(BF16)
            ebuf[m, g, pl.ds(W + o, B), cols] = (pr * w1 + pi * w0).astype(BF16)

    def left(m, g, half):
        x = dot(ltab[half * W : (half + 1) * W], ebuf[m, g]).astype(BF16)
        abuf[g, :, half * W : (half + 1) * W] = x

    def right(s, g, odd):
        on = s < live[0]
        y = dot(abuf[g], rtab[:, odd * W : (odd + 1) * W])
        for k in range(2):
            rows = slice(k * H, (k + 1) * H)
            yr, yi = y[rows, :H], y[rows, H:]
            amp = amps[s, rows, odd * H : (odd + 1) * H].astype(F32)
            f = amp * lax.rsqrt(jnp.maximum(yr * yr + yi * yi, 0.0625)) - 1.0
            f = jnp.where(on, f, 0.0)
            dbuf[g, k, :H, odd * H : (odd + 1) * H] = (f * yr).astype(BF16)
            dbuf[g, k, H:, odd * H : (odd + 1) * H] = (f * yi).astype(BF16)

    def unleft(g):
        be = dot(tab[1], dbuf[g, 0])
        bo = dot(tab[3], dbuf[g, 1])
        for sign in range(2):
            b = (be - bo if sign else be + bo).astype(BF16)
            rows = slice(sign * H, (sign + 1) * H)
            for odd in range(2):
                cols = slice(odd * H, (odd + 1) * H)
                bbuf[g, odd, rows, :H] = b[:H, cols]
                bbuf[g, odd, rows, H:] = b[H:, cols]

    def unright(m, g, odd):
        cbuf[m, g, odd] = dot(bbuf[g, odd], tab[2 * odd])

    def put(first, m, i):
        o = i * B
        rows = pl.ds(o, B)
        places = [place_of(first + g) for g in range(G)]
        terms = [[[], []] for _ in range(G)]
        for t in range(2):
            cols = slice(t * LANE, (t + 1) * LANE)
            at_re = pl.ds(t * W + o, B)
            at_im = pl.ds((2 + t) * W + o, B)
            pr = probe[at_re, :]
            pi = probe[at_im, :]
            sum_re, sum_im = pacc[at_re, :], pacc[at_im, :]
            for g in range(G):
                sh = places[g][2]
                er, ei = cbuf[m, g, 0, rows, :H], cbuf[m, g, 0, rows, H:]
                dr, di = cbuf[m, g, 1, rows, :H], cbuf[m, g, 1, rows, H:]
                cr, ci = (er - dr, ei - di) if t else (er + dr, ei + di)
                wr = win[m, g, 0, rows, cols]
                wi = win[m, g, 1, rows, cols]
                sum_re += wr * cr + wi * ci
                sum_im += wr * ci - wi * cr
                terms[g][0].append(pltpu.roll(pr * cr + pi * ci, sh, 1))
                terms[g][1].append(pltpu.roll(pr * ci - pi * cr, sh, 1))
            pacc[at_re, :] = sum_re
            pacc[at_im, :] = sum_im
        for g in range(G):
            r, q, sh = places[g]
            keep = lane >= sh
            at = pl.ds(r + o, B)
            for part in range(2):
                a, b = terms[g][part]
                acc[part, q, at, :] += jnp.where(keep, a, 0.0)
                acc[part, q + 1, at, :] += jnp.where(keep, b, a)
                acc[part, q + 2, at, :] += jnp.where(keep, 0.0, b)

    def stage(p, m):
        before = jnp.maximum(p - 1, 0)
        after = jnp.minimum(p + 1, groups - 1)
        main = []
        for g in range(G):
            main += [lambda g=g, h=h: left(m, g, h) for h in range(2)]
        for g in range(G):
            main += [lambda g=g, h=h: right(p * G + g, g, h) for h in range(2)]
        for g in range(G):
            main += [lambda g=g: unleft(g)]
        for g in range(G):
            main += [lambda g=g, h=h: unright(m, g, h) for h in range(2)]
        side = []
        for i in range(W // B):
            side.append(lambda i=i: put(before * G, 1 - m, i))
            side += [lambda g=g, i=i: form(after * G + g, 1 - m, g, i) for g in range(G)]
        done = 0
        for n, work in enumerate(main):
            work()
            upto = len(side) * (n + 1) // len(main)
            for extra in side[done:upto]:
                extra()
            done = upto

    for g in range(G):
        for i in range(W // B):
            form(g, 0, g, i)

    def step(p, _):
        stage(2 * p, 0)
        stage(2 * p + 1, 1)
        return 0

    lax.fori_loop(0, groups // 2, step, 0)
    for i in range(W // B):
        put(slots - G, 1, i)


def window_call(places, live, ext, probe, amps, ltab, rtab, tab):
    return pl.pallas_call(
        window_kernel,
        out_shape=(EXT, FLAT),
        in_specs=[SM, SM, VM, VM, VM, VM, VM, VM],
        out_specs=(VM, VM),
        scratch_shapes=[
            pltpu.VMEM((2, G, 2, W, W), F32),
            pltpu.VMEM((2, G, 2 * W, W), BF16),
            pltpu.VMEM((G, W, 2 * W), BF16),
            pltpu.VMEM((G, 2, W, W), BF16),
            pltpu.VMEM((G, 2, W, W), BF16),
            pltpu.VMEM((2, G, 2, W, W), F32),
        ],
        compiler_params=pltpu.CompilerParams(vmem_limit_bytes=VLIM),
        name="windows",
    )(places, live, ext, probe, amps, ltab, rtab, tab)


def remote(src, dst, send, recv, to):
    return pltpu.make_async_remote_copy(
        src_ref=src, dst_ref=dst, send_sem=send, recv_sem=recv, device_id=to, device_id_type=MESH
    )


def where_am_i():
    row = lax.axis_index("row")
    col = lax.axis_index("col")
    up = (lax.rem(row + ROWS - 1, ROWS), col)
    down = (lax.rem(row + 1, ROWS), col)
    west = (row, lax.rem(col + COLS - 1, COLS))
    east = (row, lax.rem(col + 1, COLS))
    return row, col, up, down, west, east


def greet(targets, meanwhile=lambda: None):
    barrier = pltpu.get_barrier_semaphore()
    for target in targets:
        pl.semaphore_signal(barrier, inc=1, device_id=target, device_id_type=MESH)
    meanwhile()
    pl.semaphore_wait(barrier, len(targets))


def pieces(bounds, base=0):
    return [pl.ds(base + first, end - first) for first, end in zip(bounds, bounds[1:])]


class Copy:
    def __init__(self, made):
        self.made, self.left = made, False
        self.start, self.wait_recv = made.start, made.wait_recv

    def wait_send(self):
        if not self.left:
            self.left = True
            self.made.wait_send()


class Links:
    def __init__(self, send, recv):
        self.send, self.recv, self.copies = send, recv, []

    def copy(self, src, dst, to):
        at = len(self.copies)
        self.copies.append(Copy(remote(src, dst, self.send.at[at], self.recv.at[at], to)))
        return self.copies[-1]

    def start(self, src, dst, to):
        made = self.copy(src, dst, to)
        made.start()
        return made

    def drain(self):
        for made in self.copies:
            made.wait_send()


def halo_copies(links, ext, bounds, west, up):
    near, far = pl.ds(0, 2), pl.ds(2, 2)
    high, low = pieces(bounds), pieces(bounds, W)
    to_west = [links.copy(ext.at[:, near, a, :], ext.at[:, far, a, :], west) for a in high]
    to_up = [links.copy(ext.at[:, near, a, :], ext.at[:, near, b, :], up) for a, b in zip(high, low)]
    onward = [links.copy(ext.at[:, far, a, :], ext.at[:, far, b, :], up) for a, b in zip(high, low)]
    return to_west, to_up, onward


HALO_SEMS = 3 * (len(FIRST) - 1)
UPDATE_SEMS = 96


def halo_kernel(obj, probe, amps, ext, flat, amps_out, amps_in, sort, send, recv, local, amp_sem):
    row, col, up, down, west, east = where_am_i()
    slots = amps.shape[0]
    inward = [
        pltpu.make_async_copy(obj.at[:, :, pl.ds(t * LANE, LANE)], ext.at[:, t, pl.ds(0, W), :], local.at[t])
        for t in range(2)
    ]
    fill = pltpu.make_async_copy(amps, amps_in, amp_sem)
    lay = [
        pltpu.make_async_copy(
            probe.at[part, :, pl.ds(t * LANE, LANE)],
            flat.at[pl.ds((part * 2 + t) * W, W), :],
            local.at[2 + part * 2 + t],
        )
        for part in range(2)
        for t in range(2)
    ]
    for copy in [*inward, fill, *lay]:
        copy.start()
    greet([up, down, west, east])
    inward[0].wait()
    inward[1].wait()
    links = Links(send, recv)
    copies = halo_copies(links, ext, FIRST, west, up)
    to_west, to_up, onward = copies
    ahead = 4
    for k in range(ahead):
        to_west[k].start()
    to_up[0].start()
    to_up[1].start()
    at = lax.broadcasted_iota(jnp.int32, (W, W), 0)
    to = lax.broadcasted_iota(jnp.int32, (W, W), 1)
    sort[...] = jnp.where(at == jnp.where(to < H, 2 * to, 2 * to + 1 - W), 1.0, 0.0).astype(BF16)
    fill.wait()

    def reorder(s):
        rows = lax.dot_general(sort[...], amps_in[s], (((0,), (0,)), ((), ())), preferred_element_type=F32)
        amps_out[s] = dot(rows.astype(BF16), sort[...]).astype(BF16)

    def reorder_some(first, last):
        def one(s, _):
            reorder(s)
            return 0

        lax.fori_loop(first, last, one, 0)

    count = len(to_west)
    for k in range(count):
        reorder_some(k * slots // count, (k + 1) * slots // count)
        to_west[k].wait_recv()
        onward[k].start()
        if k + ahead < count:
            to_west[k + ahead].start()
        if k + 2 < count:
            to_up[k + 2].start()
    for copy in [*to_up, *onward]:
        copy.wait_recv()
    for copy in lay:
        copy.wait()
    links.drain()


def halo_call(obj, probe, amps):
    return pl.pallas_call(
        halo_kernel,
        out_shape=(EXT, FLAT, jax.ShapeDtypeStruct(amps.shape, BF16)),
        in_specs=[HBM, HBM, HBM],
        out_specs=(VM, VM, VM),
        scratch_shapes=[
            pltpu.VMEM(amps.shape, BF16),
            pltpu.VMEM((W, W), BF16),
            DMA((HALO_SEMS,)),
            DMA((HALO_SEMS,)),
            DMA((6,)),
            DMA,
        ],
        compiler_params=pltpu.CompilerParams(collective_id=0, has_side_effects=True, vmem_limit_bytes=VLIM),
        name="first_halo",
    )(*(pltpu.with_memory_space_constraint(v, pltpu.HBM) for v in (obj, probe, amps)))


TOP = 16
FRAME = W + 2 * TOP


def correlate_block(v, o, kernel, slabs, lane):
    sums = []
    for t in range(3):
        above, here, below = (v(t, o + a) for a in (-1, 0, 1))
        sums.append([above * kernel(0, b) + here * kernel(1, b) + below * kernel(2, b) for b in range(3)])
    before = [pltpu.roll(sums[t][0], 1, 1) for t in range(3)]
    after = [pltpu.roll(sums[t][2], LANE - 1, 1) for t in range(3)]
    return [
        sums[t][1]
        + jnp.where(lane == 0, before[(t + 2) % 3], before[t])
        + jnp.where(lane == LANE - 1, after[(t + 1) % 3], after[t])
        for t in slabs
    ]


def update_kernel(
    step, last, acc, ext_old, pacc, flat_old, kernel_first, kernel_second, ext, flat,
    from_up, from_west, onward, strip, strip_up, strip_west, strip_on, strip_new, rim_in, corner_in, frame, real,
    p1, h1, p2, h3, p4, send, recv,
):
    row, col, up, down, west, east = where_am_i()
    core = lax.rem(row, 2)
    y = row // 2
    mate = (row + 1 - 2 * core, col)
    beyond = (lax.rem(row + ROWS - 1 + 2 * core, ROWS), col)
    in_y = [(lax.rem(row + 2 * d, ROWS), col) for d in range(1, 4)]
    in_col = [(row, lax.rem(col + d, COLS)) for d in range(1, COLS)]
    corners = [(r[0], c[1]) for r in (up, down) for c in (west, east)]
    links = Links(send, recv)
    near, far = pl.ds(0, 2), pl.ds(2, 2)
    ends = (pl.ds(0, 8), pl.ds(W - 8, 8))
    side = lax.broadcasted_iota(jnp.int32, (W, LANE), 1) < LANE // 2

    def sides_of(left, right):
        turned = jnp.where(side, left, right).T
        return jnp.concatenate([turned[:8, :], turned[LANE - 8 :, :]], axis=0)

    def acc_sides(low):
        rows = pl.ds(low * W, W)
        for part in range(2):
            for half in range(2):
                strip[low, part, half, :, :] = sides_of(acc[part, 2 * half, rows, :], acc[part, 2 * half + 1, rows, :])

    greet([mate, beyond, *in_y, *in_col, *corners], lambda: acc_sides(1))

    first_y = [links.start(strip.at[1], strip_up, down)]
    for a, b in zip(ends, (pl.ds(W, 8), pl.ds(2 * W - 8, 8))):
        first_y.append(links.start(acc.at[:, :, b, :], from_up.at[:, :, a, :], down))
    mine = pl.multiple_of(core * 512, 512)
    other = pl.multiple_of(512 - core * 512, 512)
    halves = links.start(pacc.at[pl.ds(other, 512), :], p1, mate)
    high, low = pieces(SPILL), pieces(SPILL, W)
    y_far = [links.copy(acc.at[:, far, b, :], from_up.at[:, far, a, :], down) for a, b in zip(high, low)]
    y_near = [links.copy(acc.at[:, near, b, :], from_up.at[:, near, a, :], down) for a, b in zip(high, low)]
    y_far[0].start()
    y_far[1].start()
    acc_sides(0)
    old_sides = [sides_of(ext_old[part, 0, pl.ds(0, W), :], ext_old[part, 1, pl.ds(0, W), :]) for part in range(2)]

    def join(rows):
        for part in range(2):
            for t in range(2):
                onward[part, t, rows, :] = acc[part, 2 + t, rows, :] + from_up[part, 2 + t, rows, :]

    def step_rows(rows, to):
        for part in range(2):
            for t in range(2):
                total = acc[part, t, rows, :] + from_up[part, t, rows, :] + from_west[part, t, rows, :]
                frame[part, 1 + t, to, :] = ext_old[part, t, rows, :] + total * (1.0 / 16.0)

    def over(bounds, k, size, work):
        def one(i, _):
            work(pl.multiple_of(i * size, size))
            return 0

        lax.fori_loop(bounds[k] // size, bounds[k + 1] // size, one, 0)

    x_copies = []

    def pass_on(k):
        y_far[k].wait_recv()
        over(SPILL, k, 8, lambda o: join(pl.ds(o, 8)))
        rows = pieces(SPILL)[k]
        x_copies.append(links.start(onward.at[:, :, rows, :], from_west.at[:, :, rows, :], east))

    halves.wait_recv()

    def join_half(i, _):
        o = pl.multiple_of(i * 64, 64)
        h1[pl.ds(o, 64), :] = pacc[pl.ds(mine + o, 64), :] + p1[pl.ds(o, 64), :]
        return 0

    lax.fori_loop(0, 8, join_half, 0)
    for copy in first_y:
        copy.wait_recv()
    for a in ends:
        join(a)
    for part in range(2):
        strip_on[part, :, :] = strip[0, part, 1, :, :] + strip_up[part, 1, :, :]
    first_x = [links.start(strip_on, strip_west, east)]
    for a in ends:
        first_x.append(links.start(onward.at[:, :, a, :], from_west.at[:, :, a, :], east))

    over_col = []
    for d in range(1, COLS):
        block = pl.multiple_of(lax.rem(col + d, COLS) * 32, 32)
        over_col.append(links.start(h1.at[pl.ds(block, 32), :], p2.at[d - 1], in_col[d - 1]))
    y_far[1].wait_send()
    y_far[2].start()
    y_near[0].start()
    pass_on(0)

    for copy in first_x:
        copy.wait_recv()
    for part in range(2):
        total = strip[0, part, 0, :, :] + strip_up[part, 0, :, :] + strip_west[part, :, :]
        strip_new[part, :, :] = old_sides[part] + total * (1.0 / 16.0)
    step_rows(ends[0], pl.ds(TOP, 8))
    step_rows(ends[1], pl.ds(TOP + W - 8, 8))
    top_in, top_out = pl.ds(TOP - 8, 8), pl.ds(TOP, 8)
    low_in, low_out = pl.ds(TOP + W, 8), pl.ds(TOP + W - 8, 8)
    both = pl.ds(1, 2)
    rims = [
        links.start(strip_new.at[:, pl.ds(0, 8), :], rim_in.at[0], west),
        links.start(strip_new.at[:, pl.ds(8, 8), :], rim_in.at[1], east),
        links.start(frame.at[:, both, top_out, :], frame.at[:, both, low_in, :], up),
        links.start(frame.at[:, both, low_out, :], frame.at[:, both, top_in, :], down),
        links.start(frame.at[:, 1, top_out, :], corner_in.at[0], corners[0]),
        links.start(frame.at[:, 2, top_out, :], corner_in.at[1], corners[1]),
        links.start(frame.at[:, 1, low_out, :], corner_in.at[2], corners[2]),
        links.start(frame.at[:, 2, low_out, :], corner_in.at[3], corners[3]),
    ]
    y_far[2].wait_send()
    y_far[3].start()
    y_near[1].start()
    pass_on(1)
    pass_on(2)
    y_near[2].start()
    for copy in over_col:
        copy.wait_recv()
    here = pl.multiple_of(col * 32, 32)
    total = h1[pl.ds(here, 32), :]
    for d in range(COLS - 1):
        total = total + p2[d]
    h3[...] = total
    over_y = [links.start(h3, p4.at[y], to) for to in in_y]
    p4[y] = total

    for copy in rims:
        copy.wait_recv()
    blank = jnp.zeros((LANE - 16, W), F32)
    lane8 = lax.broadcasted_iota(jnp.int32, (8, LANE), 1)
    for part in range(2):
        right_rim = jnp.where(col < COLS - 1, rim_in[0, part, :, :], 0.0)
        left_rim = jnp.where(col > 0, rim_in[1, part, :, :], 0.0)
        frame[part, 0, pl.ds(TOP, W), :] = jnp.concatenate([right_rim, blank, left_rim], axis=0).T
        for on, rows, right, left in ((row > 0, top_in, 2, 3), (row < ROWS - 1, low_in, 0, 1)):
            right_end = jnp.where(col < COLS - 1, corner_in[right, part, :, :], 0.0)
            left_end = jnp.where(col > 0, corner_in[left, part, :, :], 0.0)
            ends_in = jnp.where(lane8 < 8, right_end, jnp.where(lane8 >= LANE - 8, left_end, 0.0))
            frame[part, 0, rows, :] = jnp.where(on, ends_in, 0.0)
            for t in range(1, 3):
                frame[part, t, rows, :] = jnp.where(on, frame[part, t, rows, :], 0.0)
        for t in range(3):
            frame[part, t, pl.ds(0, 8), :] = jnp.zeros((8, LANE), F32)
            frame[part, t, pl.ds(FRAME - 8, 8), :] = jnp.zeros((8, LANE), F32)

    west_on = (col > 0).astype(F32)
    east_on = (col < COLS - 1).astype(F32)
    lane16 = lax.broadcasted_iota(jnp.int32, (16, LANE), 1)
    lane32 = lax.broadcasted_iota(jnp.int32, (32, LANE), 1)

    def tap(ref):
        return lambda a, b: ref[a, step, b]

    def first(o, count, lane, keep):
        parts = correlate_block(lambda t, at: frame[1, t, pl.ds(at, count), :], o, tap(kernel_first), range(3), lane)
        for t in range(3):
            value = frame[0, t, pl.ds(o, count), :] + jnp.tanh(parts[t])
            if t == 0:
                value = value * jnp.where(lane < LANE // 2, east_on, west_on)
            if keep is not None:
                value = value * keep
            real[t, pl.ds(o, count), :] = value

    first(TOP - 8, 8, lane8, (row > 0).astype(F32))
    first(TOP + W, 8, lane8, (row < ROWS - 1).astype(F32))

    def second(o):
        at = pl.ds(o, 32)
        o = o + TOP
        parts = correlate_block(lambda t, a: real[t, pl.ds(a, 32), :], o, tap(kernel_second), range(1, 3), lane32)
        for t in range(2):
            new_re = real[1 + t, pl.ds(o, 32), :]
            new_im = frame[1, 1 + t, pl.ds(o, 32), :] + jnp.tanh(parts[t])
            if last:
                ext[0, at, t * LANE : (t + 1) * LANE] = new_re
                ext[1, at, t * LANE : (t + 1) * LANE] = new_im
            else:
                ext[0, t, at, :] = new_re
                ext[1, t, at, :] = new_im

    if not last:
        copies = halo_copies(links, ext, LATER, west, up)

    def settle(k):
        y_near[k].wait_recv()
        x_copies[k].wait_recv()
        over(SPILL, k, 8, lambda o: step_rows(pl.ds(o, 8), pl.ds(o + TOP, 8)))
        over(REAL, k, 16, lambda o: first(o + TOP, 16, lane16, None))
        over(LATER, k, 32, second)
        if not last:
            copies[0][k].start()
            copies[1][k].start()

    for copy in over_y:
        copy.wait_recv()
    piece = pl.multiple_of(core * 512 + col * 32, 32)
    total = p4[0] + p4[1] + p4[2] + p4[3]
    flat[pl.ds(piece, 32), :] = flat_old[pl.ds(piece, 32), :] + total * (2.0 / math.sqrt(2048.0))

    def gather(first, count, targets):
        rows = pl.ds(first, count)
        return [links.start(flat.at[rows, :], flat.at[rows, :], to) for to in targets]

    back = gather(piece, 32, in_col)

    settle(0)
    pass_on(3)
    y_near[3].start()
    settle(1)
    settle(2)
    settle(3)
    for copy in back:
        copy.wait_recv()
    back = gather(mine, 512, [mate])
    if not last:
        for k in range(0, 2):
            copies[0][k].wait_recv()
            copies[2][k].start()
    if not last:
        for k in range(2, 4):
            copies[0][k].wait_recv()
            copies[2][k].start()
    if not last:
        for copy in [*copies[1], *copies[2]]:
            copy.wait_recv()
    back[0].wait_recv()
    links.drain()


def update_call(step, last, acc, ext, pacc, flat, kernel_first, kernel_second):
    return pl.pallas_call(
        functools.partial(update_kernel, step, last),
        out_shape=(TILE if last else EXT, FLAT),
        in_specs=[VM, VM, VM, VM, SM, SM],
        out_specs=(VM, VM),
        scratch_shapes=[
            pltpu.VMEM((2, 4, W, LANE), F32),
            pltpu.VMEM((2, 2, W, LANE), F32),
            pltpu.VMEM((2, 2, W, LANE), F32),
            pltpu.VMEM((2, 2, 2, 16, W), F32),
            pltpu.VMEM((2, 2, 16, W), F32),
            pltpu.VMEM((2, 16, W), F32),
            pltpu.VMEM((2, 16, W), F32),
            pltpu.VMEM((2, 16, W), F32),
            pltpu.VMEM((2, 2, 8, W), F32),
            pltpu.VMEM((4, 2, 8, LANE), F32),
            pltpu.VMEM((2, 3, FRAME, LANE), F32),
            pltpu.VMEM((3, FRAME, LANE), F32),
            pltpu.VMEM((512, LANE), F32),
            pltpu.VMEM((512, LANE), F32),
            pltpu.VMEM((COLS - 1, 32, LANE), F32),
            pltpu.VMEM((32, LANE), F32),
            pltpu.VMEM((4, 32, LANE), F32),
            DMA((UPDATE_SEMS,)),
            DMA((UPDATE_SEMS,)),
        ],
        compiler_params=pltpu.CompilerParams(
            collective_id=2 if last else 1, has_side_effects=True, vmem_limit_bytes=VLIM
        ),
        name="last_update" if last else "update",
    )(acc, ext, pacc, flat, kernel_first, kernel_second)


def body(object_field, probe, positions, amplitudes, live, kernel_first, kernel_second):
    ltab, rtab, tab = (jnp.asarray(table) for table in dft_tables())
    places = positions.T
    kernel_first = kernel_first.transpose(1, 0, 2)
    kernel_second = kernel_second.transpose(1, 0, 2)
    iters = kernel_first.shape[1]
    ext, flat, amps = halo_call(object_field, probe, amplitudes)
    for step in range(iters):
        acc, pacc = window_call(places, live, ext, flat, amps, ltab, rtab, tab)
        ext, flat = update_call(step, step == iters - 1, acc, ext, pacc, flat, kernel_first, kernel_second)
    return ext, flat.reshape(2, 2, W, LANE).transpose(0, 2, 1, 3).reshape(2, W, W)


def solution(mesh):
    return jax.shard_map(
        body,
        mesh=mesh,
        in_specs=(
            P(None, "row", "col"),
            P(),
            P(("row", "col"), None),
            P(("row", "col"), None, None),
            P(("row", "col")),
            P(),
            P(),
        ),
        out_specs=(P(None, "row", "col"), P()),
        check_vma=False,
    )
```

```python
import functools
import math

import jax
import jax.numpy as jnp
import ml_dtypes
import numpy as np
from jax import lax
from jax.experimental import pallas as pl
from jax.experimental.pallas import tpu as pltpu
from jax.sharding import PartitionSpec as P

W = 256
LANE = 128
H = W // 2
G = 2
VLIM = 32 * 2**20
ROWS = 8
COLS = 16
SPILL = (8, 96, 176, 224, 248)
FIRST = (0, 32, 64, 96, 128, 160, 192, 224, 256)
REAL = (0, 80, 160, 208, 256)
LATER = (0, 64, 128, 192, 256)
MESH = pl.DeviceIdType.MESH
F32 = jnp.float32
BF16 = jnp.bfloat16
VM = pl.BlockSpec(memory_space=pltpu.VMEM)
SM = pl.BlockSpec(memory_space=pltpu.SMEM)
HBM = pl.BlockSpec(memory_space=pltpu.HBM)
EXT = jax.ShapeDtypeStruct((2, 4, 2 * W, LANE), F32)
FLAT = jax.ShapeDtypeStruct((4 * W, LANE), F32)
TILE = jax.ShapeDtypeStruct((2, W, W), F32)
DMA = pltpu.SemaphoreType.DMA


def dft_tables():
    steps = np.arange(W)
    product = (steps[:, None] * steps[None, :]) % W
    angle = product.astype(np.float32) * np.float32(2.0 * math.pi / W)
    scale = np.float32(1.0 / math.sqrt(W))
    fr = (np.cos(angle) * scale).astype(ml_dtypes.bfloat16)
    fi = (-np.sin(angle) * scale).astype(ml_dtypes.bfloat16)
    order = np.concatenate([np.arange(0, W, 2), np.arange(1, W, 2)])
    left = np.block([[fr, -fi], [fi, fr]])[np.concatenate([order, order + W])]
    right = left.T
    right = np.concatenate([right[:, :H], right[:, W : W + H], right[:, H:W], right[:, W + H :]], axis=1)
    halves = []
    for odd in range(2):
        re, im = fr[odd::2, :H], fi[odd::2, :H]
        g = np.block([[re, -im], [im, re]])
        halves += [g, g.T]
    return np.ascontiguousarray(left), np.ascontiguousarray(right), np.stack(halves)


def dot(a, b):
    return jnp.dot(a, b, preferred_element_type=F32)


def window_kernel(pos, live, ext, probe, amps, ltab, rtab, tab, acc, pacc, win, ebuf, abuf, dbuf, bbuf, cbuf):
    slots = amps.shape[0]
    groups = slots // G

    def zero(i, _):
        rows = pl.ds(pl.multiple_of(i * 8, 8), 8)
        for part in range(2):
            for t in range(4):
                acc[part, t, rows, :] = jnp.zeros((8, LANE), F32)
        return 0

    lax.fori_loop(0, 64, zero, 0)

    def zero_probe(i, _):
        pacc[pl.ds(pl.multiple_of(i * 64, 64), 64), :] = jnp.zeros((64, LANE), F32)
        return 0

    lax.fori_loop(0, 16, zero_probe, 0)

    B = 16
    lane = lax.broadcasted_iota(jnp.int32, (B, LANE), 1)

    def place_of(s):
        r = jnp.bitwise_and(pos[0, s], W - 1)
        c = jnp.bitwise_and(pos[1, s], W - 1)
        q = c // LANE
        return r, q, c - q * LANE

    def form(s, m, g, i):
        r, q, sh = place_of(s)
        keep = lane < LANE - sh
        o = i * B
        rows = pl.ds(o, B)
        w = []
        for part in range(2):
            cuts = [pltpu.roll(ext[part, q + u, pl.ds(r + o, B), :], LANE - sh, 1) for u in range(3)]
            w.append([jnp.where(keep, cuts[t], cuts[t + 1]) for t in range(2)])
        for t in range(2):
            cols = slice(t * LANE, (t + 1) * LANE)
            w0, w1 = w[0][t], w[1][t]
            win[m, g, 0, rows, cols] = w0
            win[m, g, 1, rows, cols] = w1
            pr = probe[pl.ds(t * W + o, B), :]
            pi = probe[pl.ds((2 + t) * W + o, B), :]
            ebuf[m, g, rows, cols] = (pr * w0 - pi * w1).astype(BF16)
            ebuf[m, g, pl.ds(W + o, B), cols] = (pr * w1 + pi * w0).astype(BF16)

    def left(m, g, half):
        x = dot(ltab[half * W : (half + 1) * W], ebuf[m, g]).astype(BF16)
        abuf[g, :, half * W : (half + 1) * W] = x

    def right(s, g, odd):
        on = s < live[0]
        y = dot(abuf[g], rtab[:, odd * W : (odd + 1) * W])
        for k in range(2):
            rows = slice(k * H, (k + 1) * H)
            yr, yi = y[rows, :H], y[rows, H:]
            amp = amps[s, rows, odd * H : (odd + 1) * H].astype(F32)
            f = amp * lax.rsqrt(jnp.maximum(yr * yr + yi * yi, 0.0625)) - 1.0
            f = jnp.where(on, f, 0.0)
            dbuf[g, k, :H, odd * H : (odd + 1) * H] = (f * yr).astype(BF16)
            dbuf[g, k, H:, odd * H : (odd + 1) * H] = (f * yi).astype(BF16)

    def unleft(g):
        be = dot(tab[1], dbuf[g, 0])
        bo = dot(tab[3], dbuf[g, 1])
        for sign in range(2):
            b = (be - bo if sign else be + bo).astype(BF16)
            rows = slice(sign * H, (sign + 1) * H)
            for odd in range(2):
                cols = slice(odd * H, (odd + 1) * H)
                bbuf[g, odd, rows, :H] = b[:H, cols]
                bbuf[g, odd, rows, H:] = b[H:, cols]

    def unright(m, g, odd):
        cbuf[m, g, odd] = dot(bbuf[g, odd], tab[2 * odd])

    def put(first, m, i):
        o = i * B
        rows = pl.ds(o, B)
        places = [place_of(first + g) for g in range(G)]
        terms = [[[], []] for _ in range(G)]
        for t in range(2):
            cols = slice(t * LANE, (t + 1) * LANE)
            at_re = pl.ds(t * W + o, B)
            at_im = pl.ds((2 + t) * W + o, B)
            pr = probe[at_re, :]
            pi = probe[at_im, :]
            sum_re, sum_im = pacc[at_re, :], pacc[at_im, :]
            for g in range(G):
                sh = places[g][2]
                er, ei = cbuf[m, g, 0, rows, :H], cbuf[m, g, 0, rows, H:]
                dr, di = cbuf[m, g, 1, rows, :H], cbuf[m, g, 1, rows, H:]
                cr, ci = (er - dr, ei - di) if t else (er + dr, ei + di)
                wr = win[m, g, 0, rows, cols]
                wi = win[m, g, 1, rows, cols]
                sum_re += wr * cr + wi * ci
                sum_im += wr * ci - wi * cr
                terms[g][0].append(pltpu.roll(pr * cr + pi * ci, sh, 1))
                terms[g][1].append(pltpu.roll(pr * ci - pi * cr, sh, 1))
            pacc[at_re, :] = sum_re
            pacc[at_im, :] = sum_im
        for g in range(G):
            r, q, sh = places[g]
            keep = lane >= sh
            at = pl.ds(r + o, B)
            for part in range(2):
                a, b = terms[g][part]
                acc[part, q, at, :] += jnp.where(keep, a, 0.0)
                acc[part, q + 1, at, :] += jnp.where(keep, b, a)
                acc[part, q + 2, at, :] += jnp.where(keep, 0.0, b)

    def stage(p, m, place=True, prepare=True):
        before, after = p - 1, p + 1
        main = []
        for g in range(G):
            main += [lambda g=g, h=h: left(m, g, h) for h in range(2)]
        for g in range(G):
            main += [lambda g=g, h=h: right(p * G + g, g, h) for h in range(2)]
        for g in range(G):
            main += [lambda g=g: unleft(g)]
        for g in range(G):
            main += [lambda g=g, h=h: unright(m, g, h) for h in range(2)]
        side = []
        for i in range(W // B):
            if place:
                side.append(lambda i=i: put(before * G, 1 - m, i))
            if prepare:
                side += [lambda g=g, i=i: form(after * G + g, 1 - m, g, i) for g in range(G)]
        done = 0
        for n, work in enumerate(main):
            work()
            upto = len(side) * (n + 1) // len(main)
            for extra in side[done:upto]:
                extra()
            done = upto

    for g in range(G):
        for i in range(W // B):
            form(g, 0, g, i)

    def step(p, _):
        stage(2 * p + 1, 1)
        stage(2 * p + 2, 0)
        return 0

    stage(0, 0, place=False)
    lax.fori_loop(0, groups // 2 - 1, step, 0)
    stage(groups - 1, 1, prepare=False)
    for i in range(W // B):
        put(slots - G, 1, i)


def window_call(places, live, ext, probe, amps, ltab, rtab, tab):
    return pl.pallas_call(
        window_kernel,
        out_shape=(EXT, FLAT),
        in_specs=[SM, SM, VM, VM, VM, VM, VM, VM],
        out_specs=(VM, VM),
        scratch_shapes=[
            pltpu.VMEM((2, G, 2, W, W), F32),
            pltpu.VMEM((2, G, 2 * W, W), BF16),
            pltpu.VMEM((G, W, 2 * W), BF16),
            pltpu.VMEM((G, 2, W, W), BF16),
            pltpu.VMEM((G, 2, W, W), BF16),
            pltpu.VMEM((2, G, 2, W, W), F32),
        ],
        compiler_params=pltpu.CompilerParams(vmem_limit_bytes=VLIM),
        name="windows",
    )(places, live, ext, probe, amps, ltab, rtab, tab)


def remote(src, dst, send, recv, to):
    return pltpu.make_async_remote_copy(
        src_ref=src, dst_ref=dst, send_sem=send, recv_sem=recv, device_id=to, device_id_type=MESH
    )


def where_am_i():
    row = lax.axis_index("row")
    col = lax.axis_index("col")
    up = (lax.rem(row + ROWS - 1, ROWS), col)
    down = (lax.rem(row + 1, ROWS), col)
    west = (row, lax.rem(col + COLS - 1, COLS))
    east = (row, lax.rem(col + 1, COLS))
    return row, col, up, down, west, east


def greet(targets, meanwhile=lambda: None):
    barrier = pltpu.get_barrier_semaphore()
    for target in targets:
        pl.semaphore_signal(barrier, inc=1, device_id=target, device_id_type=MESH)
    meanwhile()
    pl.semaphore_wait(barrier, len(targets))


def pieces(bounds, base=0):
    return [pl.ds(base + first, end - first) for first, end in zip(bounds, bounds[1:])]


class Copy:
    def __init__(self, made):
        self.made, self.left = made, False
        self.start, self.wait_recv = made.start, made.wait_recv

    def wait_send(self):
        if not self.left:
            self.left = True
            self.made.wait_send()


class Links:
    def __init__(self, send, recv):
        self.send, self.recv, self.copies = send, recv, []

    def copy(self, src, dst, to):
        at = len(self.copies)
        self.copies.append(Copy(remote(src, dst, self.send.at[at], self.recv.at[at], to)))
        return self.copies[-1]

    def start(self, src, dst, to):
        made = self.copy(src, dst, to)
        made.start()
        return made

    def drain(self):
        for made in self.copies:
            made.wait_send()


def halo_copies(links, ext, bounds, west, up):
    near, far = pl.ds(0, 2), pl.ds(2, 2)
    high, low = pieces(bounds), pieces(bounds, W)
    to_west = [links.copy(ext.at[:, near, a, :], ext.at[:, far, a, :], west) for a in high]
    to_up = [links.copy(ext.at[:, near, a, :], ext.at[:, near, b, :], up) for a, b in zip(high, low)]
    onward = [links.copy(ext.at[:, far, a, :], ext.at[:, far, b, :], up) for a, b in zip(high, low)]
    return to_west, to_up, onward


HALO_SEMS = 3 * (len(FIRST) - 1)
UPDATE_SEMS = 96


def halo_kernel(obj, probe, amps, ext, flat, amps_out, amps_in, sort, send, recv, local, amp_sem):
    row, col, up, down, west, east = where_am_i()
    slots = amps.shape[0]
    inward = [
        pltpu.make_async_copy(obj.at[:, :, pl.ds(t * LANE, LANE)], ext.at[:, t, pl.ds(0, W), :], local.at[t])
        for t in range(2)
    ]
    fill = pltpu.make_async_copy(amps, amps_in, amp_sem)
    lay = [
        pltpu.make_async_copy(
            probe.at[part, :, pl.ds(t * LANE, LANE)],
            flat.at[pl.ds((part * 2 + t) * W, W), :],
            local.at[2 + part * 2 + t],
        )
        for part in range(2)
        for t in range(2)
    ]
    for copy in [*inward, fill, *lay]:
        copy.start()
    greet([up, down, west, east])
    inward[0].wait()
    inward[1].wait()
    links = Links(send, recv)
    copies = halo_copies(links, ext, FIRST, west, up)
    to_west, to_up, onward = copies
    ahead = 4
    for k in range(ahead):
        to_west[k].start()
    to_up[0].start()
    to_up[1].start()
    at = lax.broadcasted_iota(jnp.int32, (W, W), 0)
    to = lax.broadcasted_iota(jnp.int32, (W, W), 1)
    sort[...] = jnp.where(at == jnp.where(to < H, 2 * to, 2 * to + 1 - W), 1.0, 0.0).astype(BF16)
    fill.wait()

    def reorder(s):
        rows = lax.dot_general(sort[...], amps_in[s], (((0,), (0,)), ((), ())), preferred_element_type=F32)
        amps_out[s] = dot(rows.astype(BF16), sort[...]).astype(BF16)

    def reorder_some(first, last):
        def one(s, _):
            reorder(s)
            return 0

        lax.fori_loop(first, last, one, 0)

    count = len(to_west)
    for k in range(count):
        reorder_some(k * slots // count, (k + 1) * slots // count)
        to_west[k].wait_recv()
        onward[k].start()
        if k + ahead < count:
            to_west[k + ahead].start()
        if k + 2 < count:
            to_up[k + 2].start()
    for copy in [*to_up, *onward]:
        copy.wait_recv()
    for copy in lay:
        copy.wait()
    links.drain()


def halo_call(obj, probe, amps):
    return pl.pallas_call(
        halo_kernel,
        out_shape=(EXT, FLAT, jax.ShapeDtypeStruct(amps.shape, BF16)),
        in_specs=[HBM, HBM, HBM],
        out_specs=(VM, VM, VM),
        scratch_shapes=[
            pltpu.VMEM(amps.shape, BF16),
            pltpu.VMEM((W, W), BF16),
            DMA((HALO_SEMS,)),
            DMA((HALO_SEMS,)),
            DMA((6,)),
            DMA,
        ],
        compiler_params=pltpu.CompilerParams(collective_id=0, has_side_effects=True, vmem_limit_bytes=VLIM),
        name="first_halo",
    )(*(pltpu.with_memory_space_constraint(v, pltpu.HBM) for v in (obj, probe, amps)))


TOP = 16
FRAME = W + 2 * TOP


def correlate_block(v, o, kernel, slabs, lane):
    sums = []
    for t in range(3):
        above, here, below = (v(t, o + a) for a in (-1, 0, 1))
        sums.append([above * kernel(0, b) + here * kernel(1, b) + below * kernel(2, b) for b in range(3)])
    before = [pltpu.roll(sums[t][0], 1, 1) for t in range(3)]
    after = [pltpu.roll(sums[t][2], LANE - 1, 1) for t in range(3)]
    return [
        sums[t][1]
        + jnp.where(lane == 0, before[(t + 2) % 3], before[t])
        + jnp.where(lane == LANE - 1, after[(t + 1) % 3], after[t])
        for t in slabs
    ]


def update_kernel(
    step, last, acc, ext_old, pacc, flat_old, kernel_first, kernel_second, ext, flat,
    from_up, from_west, onward, strip, strip_up, strip_west, strip_on, strip_new, rim_in, corner_in, frame, real,
    p1, h1, p2, h3, p4, send, recv,
):
    row, col, up, down, west, east = where_am_i()
    core = lax.rem(row, 2)
    y = row // 2
    mate = (row + 1 - 2 * core, col)
    beyond = (lax.rem(row + ROWS - 1 + 2 * core, ROWS), col)
    in_y = [(lax.rem(row + 2 * d, ROWS), col) for d in range(1, 4)]
    in_col = [(row, lax.rem(col + d, COLS)) for d in range(1, COLS)]
    corners = [(r[0], c[1]) for r in (up, down) for c in (west, east)]
    links = Links(send, recv)
    near, far = pl.ds(0, 2), pl.ds(2, 2)
    ends = (pl.ds(0, 8), pl.ds(W - 8, 8))
    side = lax.broadcasted_iota(jnp.int32, (W, LANE), 1) < LANE // 2

    def sides_of(left, right):
        turned = jnp.where(side, left, right).T
        return jnp.concatenate([turned[:8, :], turned[LANE - 8 :, :]], axis=0)

    def acc_sides(low):
        rows = pl.ds(low * W, W)
        for part in range(2):
            for half in range(2):
                strip[low, part, half, :, :] = sides_of(acc[part, 2 * half, rows, :], acc[part, 2 * half + 1, rows, :])

    greet([mate, beyond, *in_y, *in_col, *corners], lambda: acc_sides(1))

    first_y = [links.start(strip.at[1], strip_up, down)]
    for a, b in zip(ends, (pl.ds(W, 8), pl.ds(2 * W - 8, 8))):
        first_y.append(links.start(acc.at[:, :, b, :], from_up.at[:, :, a, :], down))
    mine = pl.multiple_of(core * 512, 512)
    other = pl.multiple_of(512 - core * 512, 512)
    halves = links.start(pacc.at[pl.ds(other, 512), :], p1, mate)
    high, low = pieces(SPILL), pieces(SPILL, W)
    y_far = [links.copy(acc.at[:, far, b, :], from_up.at[:, far, a, :], down) for a, b in zip(high, low)]
    y_near = [links.copy(acc.at[:, near, b, :], from_up.at[:, near, a, :], down) for a, b in zip(high, low)]
    y_far[0].start()
    y_far[1].start()
    acc_sides(0)
    old_sides = [sides_of(ext_old[part, 0, pl.ds(0, W), :], ext_old[part, 1, pl.ds(0, W), :]) for part in range(2)]

    def join(rows):
        for part in range(2):
            for t in range(2):
                onward[part, t, rows, :] = acc[part, 2 + t, rows, :] + from_up[part, 2 + t, rows, :]

    def step_rows(rows, to):
        for part in range(2):
            for t in range(2):
                total = acc[part, t, rows, :] + from_up[part, t, rows, :] + from_west[part, t, rows, :]
                frame[part, 1 + t, to, :] = ext_old[part, t, rows, :] + total * (1.0 / 16.0)

    def over(bounds, k, size, work):
        def one(i, _):
            work(pl.multiple_of(i * size, size))
            return 0

        lax.fori_loop(bounds[k] // size, bounds[k + 1] // size, one, 0)

    x_copies = []

    def pass_on(k):
        y_far[k].wait_recv()
        over(SPILL, k, 8, lambda o: join(pl.ds(o, 8)))
        rows = pieces(SPILL)[k]
        x_copies.append(links.start(onward.at[:, :, rows, :], from_west.at[:, :, rows, :], east))

    for copy in first_y:
        copy.wait_recv()
    for a in ends:
        join(a)
    for part in range(2):
        strip_on[part, :, :] = strip[0, part, 1, :, :] + strip_up[part, 1, :, :]
    first_x = [links.start(strip_on, strip_west, east)]
    for a in ends:
        first_x.append(links.start(onward.at[:, :, a, :], from_west.at[:, :, a, :], east))

    halves.wait_recv()

    def join_half(i, _):
        o = pl.multiple_of(i * 64, 64)
        h1[pl.ds(o, 64), :] = pacc[pl.ds(mine + o, 64), :] + p1[pl.ds(o, 64), :]
        return 0

    lax.fori_loop(0, 8, join_half, 0)
    over_col = []
    for d in range(1, COLS):
        block = pl.multiple_of(lax.rem(col + d, COLS) * 32, 32)
        over_col.append(links.start(h1.at[pl.ds(block, 32), :], p2.at[d - 1], in_col[d - 1]))
    y_far[1].wait_send()
    y_far[2].start()
    y_near[0].start()
    pass_on(0)

    for copy in first_x:
        copy.wait_recv()
    for part in range(2):
        total = strip[0, part, 0, :, :] + strip_up[part, 0, :, :] + strip_west[part, :, :]
        strip_new[part, :, :] = old_sides[part] + total * (1.0 / 16.0)
    step_rows(ends[0], pl.ds(TOP, 8))
    step_rows(ends[1], pl.ds(TOP + W - 8, 8))
    top_in, top_out = pl.ds(TOP - 8, 8), pl.ds(TOP, 8)
    low_in, low_out = pl.ds(TOP + W, 8), pl.ds(TOP + W - 8, 8)
    both = pl.ds(1, 2)
    rims = [
        links.start(strip_new.at[:, pl.ds(0, 8), :], rim_in.at[0], west),
        links.start(strip_new.at[:, pl.ds(8, 8), :], rim_in.at[1], east),
        links.start(frame.at[:, both, top_out, :], frame.at[:, both, low_in, :], up),
        links.start(frame.at[:, both, low_out, :], frame.at[:, both, top_in, :], down),
        links.start(frame.at[:, 1, top_out, :], corner_in.at[0], corners[0]),
        links.start(frame.at[:, 2, top_out, :], corner_in.at[1], corners[1]),
        links.start(frame.at[:, 1, low_out, :], corner_in.at[2], corners[2]),
        links.start(frame.at[:, 2, low_out, :], corner_in.at[3], corners[3]),
    ]
    y_far[2].wait_send()
    y_far[3].start()
    y_near[1].start()
    pass_on(1)
    pass_on(2)
    y_near[2].start()
    for copy in over_col:
        copy.wait_recv()
    here = pl.multiple_of(col * 32, 32)
    total = h1[pl.ds(here, 32), :]
    for d in range(COLS - 1):
        total = total + p2[d]
    h3[...] = total
    over_y = [links.start(h3, p4.at[y], to) for to in in_y]
    p4[y] = total

    for copy in rims:
        copy.wait_recv()
    blank = jnp.zeros((LANE - 16, W), F32)
    lane8 = lax.broadcasted_iota(jnp.int32, (8, LANE), 1)
    for part in range(2):
        right_rim = jnp.where(col < COLS - 1, rim_in[0, part, :, :], 0.0)
        left_rim = jnp.where(col > 0, rim_in[1, part, :, :], 0.0)
        frame[part, 0, pl.ds(TOP, W), :] = jnp.concatenate([right_rim, blank, left_rim], axis=0).T
        for on, rows, right, left in ((row > 0, top_in, 2, 3), (row < ROWS - 1, low_in, 0, 1)):
            right_end = jnp.where(col < COLS - 1, corner_in[right, part, :, :], 0.0)
            left_end = jnp.where(col > 0, corner_in[left, part, :, :], 0.0)
            ends_in = jnp.where(lane8 < 8, right_end, jnp.where(lane8 >= LANE - 8, left_end, 0.0))
            frame[part, 0, rows, :] = jnp.where(on, ends_in, 0.0)
            for t in range(1, 3):
                frame[part, t, rows, :] = jnp.where(on, frame[part, t, rows, :], 0.0)
        for t in range(3):
            frame[part, t, pl.ds(0, 8), :] = jnp.zeros((8, LANE), F32)
            frame[part, t, pl.ds(FRAME - 8, 8), :] = jnp.zeros((8, LANE), F32)

    west_on = (col > 0).astype(F32)
    east_on = (col < COLS - 1).astype(F32)
    lane16 = lax.broadcasted_iota(jnp.int32, (16, LANE), 1)
    lane32 = lax.broadcasted_iota(jnp.int32, (32, LANE), 1)

    def tap(ref):
        return lambda a, b: ref[a, step, b]

    def first(o, count, lane, keep):
        parts = correlate_block(lambda t, at: frame[1, t, pl.ds(at, count), :], o, tap(kernel_first), range(3), lane)
        for t in range(3):
            value = frame[0, t, pl.ds(o, count), :] + jnp.tanh(parts[t])
            if t == 0:
                value = value * jnp.where(lane < LANE // 2, east_on, west_on)
            if keep is not None:
                value = value * keep
            real[t, pl.ds(o, count), :] = value

    first(TOP - 8, 8, lane8, (row > 0).astype(F32))
    first(TOP + W, 8, lane8, (row < ROWS - 1).astype(F32))

    def second(o):
        at = pl.ds(o, 32)
        o = o + TOP
        parts = correlate_block(lambda t, a: real[t, pl.ds(a, 32), :], o, tap(kernel_second), range(1, 3), lane32)
        for t in range(2):
            new_re = real[1 + t, pl.ds(o, 32), :]
            new_im = frame[1, 1 + t, pl.ds(o, 32), :] + jnp.tanh(parts[t])
            if last:
                ext[0, at, t * LANE : (t + 1) * LANE] = new_re
                ext[1, at, t * LANE : (t + 1) * LANE] = new_im
            else:
                ext[0, t, at, :] = new_re
                ext[1, t, at, :] = new_im

    if not last:
        copies = halo_copies(links, ext, LATER, west, up)

    def settle(k):
        y_near[k].wait_recv()
        x_copies[k].wait_recv()
        over(SPILL, k, 8, lambda o: step_rows(pl.ds(o, 8), pl.ds(o + TOP, 8)))
        over(REAL, k, 16, lambda o: first(o + TOP, 16, lane16, None))
        over(LATER, k, 32, second)
        if not last:
            copies[0][k].start()
            copies[1][k].start()

    for copy in over_y:
        copy.wait_recv()
    piece = pl.multiple_of(core * 512 + col * 32, 32)
    total = p4[0] + p4[1] + p4[2] + p4[3]
    flat[pl.ds(piece, 32), :] = flat_old[pl.ds(piece, 32), :] + total * (2.0 / math.sqrt(2048.0))

    def gather(first, count, targets):
        rows = pl.ds(first, count)
        return [links.start(flat.at[rows, :], flat.at[rows, :], to) for to in targets]

    back = gather(piece, 32, in_col)

    settle(0)
    pass_on(3)
    y_near[3].start()
    settle(1)
    settle(2)
    for copy in back:
        copy.wait_recv()
    back = gather(mine, 512, [mate])
    settle(3)
    if not last:
        for k in range(0, 2):
            copies[0][k].wait_recv()
            copies[2][k].start()
    if not last:
        for k in range(2, 4):
            copies[0][k].wait_recv()
            copies[2][k].start()
    if not last:
        for copy in [*copies[1], *copies[2]]:
            copy.wait_recv()
    back[0].wait_recv()
    links.drain()


def update_call(step, last, acc, ext, pacc, flat, kernel_first, kernel_second):
    return pl.pallas_call(
        functools.partial(update_kernel, step, last),
        out_shape=(TILE if last else EXT, FLAT),
        in_specs=[VM, VM, VM, VM, SM, SM],
        out_specs=(VM, VM),
        scratch_shapes=[
            pltpu.VMEM((2, 4, W, LANE), F32),
            pltpu.VMEM((2, 2, W, LANE), F32),
            pltpu.VMEM((2, 2, W, LANE), F32),
            pltpu.VMEM((2, 2, 2, 16, W), F32),
            pltpu.VMEM((2, 2, 16, W), F32),
            pltpu.VMEM((2, 16, W), F32),
            pltpu.VMEM((2, 16, W), F32),
            pltpu.VMEM((2, 16, W), F32),
            pltpu.VMEM((2, 2, 8, W), F32),
            pltpu.VMEM((4, 2, 8, LANE), F32),
            pltpu.VMEM((2, 3, FRAME, LANE), F32),
            pltpu.VMEM((3, FRAME, LANE), F32),
            pltpu.VMEM((512, LANE), F32),
            pltpu.VMEM((512, LANE), F32),
            pltpu.VMEM((COLS - 1, 32, LANE), F32),
            pltpu.VMEM((32, LANE), F32),
            pltpu.VMEM((4, 32, LANE), F32),
            DMA((UPDATE_SEMS,)),
            DMA((UPDATE_SEMS,)),
        ],
        compiler_params=pltpu.CompilerParams(
            collective_id=2 if last else 1, has_side_effects=True, vmem_limit_bytes=VLIM
        ),
        name="last_update" if last else "update",
    )(acc, ext, pacc, flat, kernel_first, kernel_second)


def body(object_field, probe, positions, amplitudes, live, kernel_first, kernel_second):
    ltab, rtab, tab = (jnp.asarray(table) for table in dft_tables())
    places = positions.T
    kernel_first = kernel_first.transpose(1, 0, 2)
    kernel_second = kernel_second.transpose(1, 0, 2)
    iters = kernel_first.shape[1]
    ext, flat, amps = halo_call(object_field, probe, amplitudes)
    for step in range(iters):
        acc, pacc = window_call(places, live, ext, flat, amps, ltab, rtab, tab)
        ext, flat = update_call(step, step == iters - 1, acc, ext, pacc, flat, kernel_first, kernel_second)
    return ext, flat.reshape(2, 2, W, LANE).transpose(0, 2, 1, 3).reshape(2, W, W)


def solution(mesh):
    return jax.shard_map(
        body,
        mesh=mesh,
        in_specs=(
            P(None, "row", "col"),
            P(),
            P(("row", "col"), None),
            P(("row", "col"), None, None),
            P(("row", "col")),
            P(),
            P(),
        ),
        out_specs=(P(None, "row", "col"), P()),
        check_vma=False,
    )
```

```python
import functools
import math

import jax
import jax.numpy as jnp
import ml_dtypes
import numpy as np
from jax import lax
from jax.experimental import pallas as pl
from jax.experimental.pallas import tpu as pltpu
from jax.sharding import PartitionSpec as P

W = 256
LANE = 128
H = W // 2
G = 2
VLIM = 32 * 2**20
ROWS = 8
COLS = 16
SPILL = (8, 96, 176, 224, 248)
FIRST = (0, 32, 64, 96, 128, 160, 192, 224, 256)
REAL = (0, 80, 160, 208, 256)
LATER = (0, 64, 128, 192, 256)
MESH = pl.DeviceIdType.MESH
F32 = jnp.float32
BF16 = jnp.bfloat16
VM = pl.BlockSpec(memory_space=pltpu.VMEM)
SM = pl.BlockSpec(memory_space=pltpu.SMEM)
HBM = pl.BlockSpec(memory_space=pltpu.HBM)
EXT = jax.ShapeDtypeStruct((2, 4, 2 * W, LANE), F32)
FLAT = jax.ShapeDtypeStruct((4 * W, LANE), F32)
TILE = jax.ShapeDtypeStruct((2, W, W), F32)
DMA = pltpu.SemaphoreType.DMA


def dft_tables():
    steps = np.arange(W)
    product = (steps[:, None] * steps[None, :]) % W
    angle = product.astype(np.float32) * np.float32(2.0 * math.pi / W)
    scale = np.float32(1.0 / math.sqrt(W))
    fr = (np.cos(angle) * scale).astype(ml_dtypes.bfloat16)
    fi = (-np.sin(angle) * scale).astype(ml_dtypes.bfloat16)
    order = np.concatenate([np.arange(0, W, 2), np.arange(1, W, 2)])
    left = np.block([[fr, -fi], [fi, fr]])[np.concatenate([order, order + W])]
    right = left.T
    right = np.concatenate([right[:, :H], right[:, W : W + H], right[:, H:W], right[:, W + H :]], axis=1)
    halves = []
    for odd in range(2):
        re, im = fr[odd::2, :H], fi[odd::2, :H]
        g = np.block([[re, -im], [im, re]])
        halves += [g, g.T]
    return np.ascontiguousarray(left), np.ascontiguousarray(right), np.stack(halves)


def dot(a, b):
    return jnp.dot(a, b, preferred_element_type=F32)


def window_kernel(pos, live, ext, probe, amps, ltab, rtab, tab, acc, pacc, win, ebuf, abuf, dbuf, bbuf, cbuf):
    slots = amps.shape[0]
    groups = slots // G

    def zero(i, _):
        rows = pl.ds(pl.multiple_of(i * 8, 8), 8)
        for part in range(2):
            for t in range(4):
                acc[part, t, rows, :] = jnp.zeros((8, LANE), F32)
        return 0

    lax.fori_loop(0, 64, zero, 0)

    def zero_probe(i, _):
        pacc[pl.ds(pl.multiple_of(i * 64, 64), 64), :] = jnp.zeros((64, LANE), F32)
        return 0

    lax.fori_loop(0, 16, zero_probe, 0)

    B = 16
    lane = lax.broadcasted_iota(jnp.int32, (B, LANE), 1)

    def place_of(s):
        r = jnp.bitwise_and(pos[0, s], W - 1)
        c = jnp.bitwise_and(pos[1, s], W - 1)
        q = c // LANE
        return r, q, c - q * LANE

    def form(s, m, g, i):
        r, q, sh = place_of(s)
        keep = lane < LANE - sh
        o = i * B
        rows = pl.ds(o, B)
        w = []
        for part in range(2):
            cuts = [pltpu.roll(ext[part, q + u, pl.ds(r + o, B), :], LANE - sh, 1) for u in range(3)]
            w.append([jnp.where(keep, cuts[t], cuts[t + 1]) for t in range(2)])
        for t in range(2):
            cols = slice(t * LANE, (t + 1) * LANE)
            w0, w1 = w[0][t], w[1][t]
            win[m, g, 0, rows, cols] = w0
            win[m, g, 1, rows, cols] = w1
            pr = probe[pl.ds(t * W + o, B), :]
            pi = probe[pl.ds((2 + t) * W + o, B), :]
            ebuf[m, g, rows, cols] = (pr * w0 - pi * w1).astype(BF16)
            ebuf[m, g, pl.ds(W + o, B), cols] = (pr * w1 + pi * w0).astype(BF16)

    def left(m, g, half):
        x = dot(ltab[half * W : (half + 1) * W], ebuf[m, g]).astype(BF16)
        abuf[g, :, half * W : (half + 1) * W] = x

    def right(s, g, odd):
        on = s < live[0]
        y = dot(abuf[g], rtab[:, odd * W : (odd + 1) * W])
        for k in range(2):
            rows = slice(k * H, (k + 1) * H)
            yr, yi = y[rows, :H], y[rows, H:]
            amp = amps[s, rows, odd * H : (odd + 1) * H].astype(F32)
            f = amp * lax.rsqrt(jnp.maximum(yr * yr + yi * yi, 0.0625)) - 1.0
            f = jnp.where(on, f, 0.0)
            dbuf[g, k, :H, odd * H : (odd + 1) * H] = (f * yr).astype(BF16)
            dbuf[g, k, H:, odd * H : (odd + 1) * H] = (f * yi).astype(BF16)

    def unleft(g):
        be = dot(tab[1], dbuf[g, 0])
        bo = dot(tab[3], dbuf[g, 1])
        for sign in range(2):
            b = (be - bo if sign else be + bo).astype(BF16)
            rows = slice(sign * H, (sign + 1) * H)
            for odd in range(2):
                cols = slice(odd * H, (odd + 1) * H)
                bbuf[g, odd, rows, :H] = b[:H, cols]
                bbuf[g, odd, rows, H:] = b[H:, cols]

    def unright(m, g, odd):
        cbuf[m, g, odd] = dot(bbuf[g, odd], tab[2 * odd])

    def put(first, m, i):
        o = i * B
        rows = pl.ds(o, B)
        places = [place_of(first + g) for g in range(G)]
        terms = [[[], []] for _ in range(G)]
        for t in range(2):
            cols = slice(t * LANE, (t + 1) * LANE)
            at_re = pl.ds(t * W + o, B)
            at_im = pl.ds((2 + t) * W + o, B)
            pr = probe[at_re, :]
            pi = probe[at_im, :]
            sum_re, sum_im = pacc[at_re, :], pacc[at_im, :]
            for g in range(G):
                sh = places[g][2]
                er, ei = cbuf[m, g, 0, rows, :H], cbuf[m, g, 0, rows, H:]
                dr, di = cbuf[m, g, 1, rows, :H], cbuf[m, g, 1, rows, H:]
                cr, ci = (er - dr, ei - di) if t else (er + dr, ei + di)
                wr = win[m, g, 0, rows, cols]
                wi = win[m, g, 1, rows, cols]
                sum_re += wr * cr + wi * ci
                sum_im += wr * ci - wi * cr
                terms[g][0].append(pltpu.roll(pr * cr + pi * ci, sh, 1))
                terms[g][1].append(pltpu.roll(pr * ci - pi * cr, sh, 1))
            pacc[at_re, :] = sum_re
            pacc[at_im, :] = sum_im
        for g in range(G):
            r, q, sh = places[g]
            keep = lane >= sh
            at = pl.ds(r + o, B)
            for part in range(2):
                a, b = terms[g][part]
                acc[part, q, at, :] += jnp.where(keep, a, 0.0)
                acc[part, q + 1, at, :] += jnp.where(keep, b, a)
                acc[part, q + 2, at, :] += jnp.where(keep, 0.0, b)

    def stage(p, m, place=True, prepare=True):
        before, after = p - 1, p + 1
        main = []
        for g in range(G):
            main += [lambda g=g, h=h: left(m, g, h) for h in range(2)]
        for g in range(G):
            main += [lambda g=g, h=h: right(p * G + g, g, h) for h in range(2)]
        for g in range(G):
            main += [lambda g=g: unleft(g)]
        for g in range(G):
            main += [lambda g=g, h=h: unright(m, g, h) for h in range(2)]
        side = []
        for i in range(W // B):
            if place:
                side.append(lambda i=i: put(before * G, 1 - m, i))
            if prepare:
                side += [lambda g=g, i=i: form(after * G + g, 1 - m, g, i) for g in range(G)]
        done = 0
        for n, work in enumerate(main):
            work()
            upto = len(side) * (n + 1) // len(main)
            for extra in side[done:upto]:
                extra()
            done = upto

    for g in range(G):
        for i in range(W // B):
            form(g, 0, g, i)

    def step(p, _):
        stage(2 * p + 1, 1)
        stage(2 * p + 2, 0)
        return 0

    stage(0, 0, place=False)
    lax.fori_loop(0, groups // 2 - 1, step, 0)
    stage(groups - 1, 1, prepare=False)
    for i in range(W // B):
        put(slots - G, 1, i)


def window_call(places, live, ext, probe, amps, ltab, rtab, tab):
    return pl.pallas_call(
        window_kernel,
        out_shape=(EXT, FLAT),
        in_specs=[SM, SM, VM, VM, VM, VM, VM, VM],
        out_specs=(VM, VM),
        scratch_shapes=[
            pltpu.VMEM((2, G, 2, W, W), F32),
            pltpu.VMEM((2, G, 2 * W, W), BF16),
            pltpu.VMEM((G, W, 2 * W), BF16),
            pltpu.VMEM((G, 2, W, W), BF16),
            pltpu.VMEM((G, 2, W, W), BF16),
            pltpu.VMEM((2, G, 2, W, W), F32),
        ],
        compiler_params=pltpu.CompilerParams(vmem_limit_bytes=VLIM),
        name="windows",
    )(places, live, ext, probe, amps, ltab, rtab, tab)


def remote(src, dst, send, recv, to):
    return pltpu.make_async_remote_copy(
        src_ref=src, dst_ref=dst, send_sem=send, recv_sem=recv, device_id=to, device_id_type=MESH
    )


def where_am_i():
    row = lax.axis_index("row")
    col = lax.axis_index("col")
    up = (lax.rem(row + ROWS - 1, ROWS), col)
    down = (lax.rem(row + 1, ROWS), col)
    west = (row, lax.rem(col + COLS - 1, COLS))
    east = (row, lax.rem(col + 1, COLS))
    return row, col, up, down, west, east


def greet(targets, meanwhile=lambda: None):
    barrier = pltpu.get_barrier_semaphore()
    for target in targets:
        pl.semaphore_signal(barrier, inc=1, device_id=target, device_id_type=MESH)
    meanwhile()
    pl.semaphore_wait(barrier, len(targets))


def pieces(bounds, base=0):
    return [pl.ds(base + first, end - first) for first, end in zip(bounds, bounds[1:])]


class Copy:
    def __init__(self, made):
        self.made, self.left = made, False
        self.start, self.wait_recv = made.start, made.wait_recv

    def wait_send(self):
        if not self.left:
            self.left = True
            self.made.wait_send()


class Links:
    def __init__(self, send, recv):
        self.send, self.recv, self.copies = send, recv, []

    def copy(self, src, dst, to):
        at = len(self.copies)
        self.copies.append(Copy(remote(src, dst, self.send.at[at], self.recv.at[at], to)))
        return self.copies[-1]

    def start(self, src, dst, to):
        made = self.copy(src, dst, to)
        made.start()
        return made

    def drain(self):
        for made in self.copies:
            made.wait_send()


def halo_copies(links, ext, bounds, west, up):
    near, far = pl.ds(0, 2), pl.ds(2, 2)
    high, low = pieces(bounds), pieces(bounds, W)
    to_west = [links.copy(ext.at[:, near, a, :], ext.at[:, far, a, :], west) for a in high]
    to_up = [links.copy(ext.at[:, near, a, :], ext.at[:, near, b, :], up) for a, b in zip(high, low)]
    onward = [links.copy(ext.at[:, far, a, :], ext.at[:, far, b, :], up) for a, b in zip(high, low)]
    return to_west, to_up, onward


HALO_SEMS = 3 * (len(FIRST) - 1)
UPDATE_SEMS = 96


def halo_kernel(obj, probe, amps, ext, flat, amps_out, amps_in, sort, send, recv, local, amp_sem):
    row, col, up, down, west, east = where_am_i()
    slots = amps.shape[0]
    inward = [
        pltpu.make_async_copy(obj.at[:, :, pl.ds(t * LANE, LANE)], ext.at[:, t, pl.ds(0, W), :], local.at[t])
        for t in range(2)
    ]
    fill = pltpu.make_async_copy(amps, amps_in, amp_sem)
    lay = [
        pltpu.make_async_copy(
            probe.at[part, :, pl.ds(t * LANE, LANE)],
            flat.at[pl.ds((part * 2 + t) * W, W), :],
            local.at[2 + part * 2 + t],
        )
        for part in range(2)
        for t in range(2)
    ]
    for copy in [*inward, fill, *lay]:
        copy.start()
    greet([up, down, west, east])
    inward[0].wait()
    inward[1].wait()
    links = Links(send, recv)
    copies = halo_copies(links, ext, FIRST, west, up)
    to_west, to_up, onward = copies
    ahead = 4
    for k in range(ahead):
        to_west[k].start()
    to_up[0].start()
    to_up[1].start()
    at = lax.broadcasted_iota(jnp.int32, (W, W), 0)
    to = lax.broadcasted_iota(jnp.int32, (W, W), 1)
    sort[...] = jnp.where(at == jnp.where(to < H, 2 * to, 2 * to + 1 - W), 1.0, 0.0).astype(BF16)
    fill.wait()

    def reorder(s):
        rows = lax.dot_general(sort[...], amps_in[s], (((0,), (0,)), ((), ())), preferred_element_type=F32)
        amps_out[s] = dot(rows.astype(BF16), sort[...]).astype(BF16)

    def reorder_some(first, last):
        def one(s, _):
            reorder(s)
            return 0

        lax.fori_loop(first, last, one, 0)

    count = len(to_west)
    for k in range(count):
        reorder_some(k * slots // count, (k + 1) * slots // count)
        to_west[k].wait_recv()
        onward[k].start()
        if k + ahead < count:
            to_west[k + ahead].start()
        if k + 2 < count:
            to_up[k + 2].start()
    for copy in [*to_up, *onward]:
        copy.wait_recv()
    for copy in lay:
        copy.wait()
    links.drain()


def halo_call(obj, probe, amps):
    return pl.pallas_call(
        halo_kernel,
        out_shape=(EXT, FLAT, jax.ShapeDtypeStruct(amps.shape, BF16)),
        in_specs=[HBM, HBM, HBM],
        out_specs=(VM, VM, VM),
        scratch_shapes=[
            pltpu.VMEM(amps.shape, BF16),
            pltpu.VMEM((W, W), BF16),
            DMA((HALO_SEMS,)),
            DMA((HALO_SEMS,)),
            DMA((6,)),
            DMA,
        ],
        compiler_params=pltpu.CompilerParams(collective_id=0, has_side_effects=True, vmem_limit_bytes=VLIM),
        name="first_halo",
    )(*(pltpu.with_memory_space_constraint(v, pltpu.HBM) for v in (obj, probe, amps)))


TOP = 16
FRAME = W + 2 * TOP


def correlate_block(v, o, kernel, slabs, lane):
    sums = []
    for t in range(3):
        above, here, below = (v(t, o + a) for a in (-1, 0, 1))
        sums.append([above * kernel(0, b) + here * kernel(1, b) + below * kernel(2, b) for b in range(3)])
    before = [pltpu.roll(sums[t][0], 1, 1) for t in range(3)]
    after = [pltpu.roll(sums[t][2], LANE - 1, 1) for t in range(3)]
    return [
        sums[t][1]
        + jnp.where(lane == 0, before[(t + 2) % 3], before[t])
        + jnp.where(lane == LANE - 1, after[(t + 1) % 3], after[t])
        for t in slabs
    ]


def update_kernel(
    step, last, acc, ext_old, pacc, flat_old, kernel_first, kernel_second, ext, flat,
    from_up, from_west, onward, strip, strip_up, strip_west, strip_on, strip_new, rim_in, corner_in, frame, real,
    p1, h1, p2, h3, p4, send, recv,
):
    row, col, up, down, west, east = where_am_i()
    core = lax.rem(row, 2)
    y = row // 2
    mate = (row + 1 - 2 * core, col)
    beyond = (lax.rem(row + ROWS - 1 + 2 * core, ROWS), col)
    in_y = [(lax.rem(row + 2 * d, ROWS), col) for d in range(1, 4)]
    in_col = [(row, lax.rem(col + d, COLS)) for d in range(1, COLS)]
    corners = [(r[0], c[1]) for r in (up, down) for c in (west, east)]
    links = Links(send, recv)
    near, far = pl.ds(0, 2), pl.ds(2, 2)
    ends = (pl.ds(0, 8), pl.ds(W - 8, 8))
    side = lax.broadcasted_iota(jnp.int32, (W, LANE), 1) < LANE // 2

    def sides_of(left, right):
        turned = jnp.where(side, left, right).T
        return jnp.concatenate([turned[:8, :], turned[LANE - 8 :, :]], axis=0)

    def acc_sides(low):
        rows = pl.ds(low * W, W)
        for part in range(2):
            for half in range(2):
                strip[low, part, half, :, :] = sides_of(acc[part, 2 * half, rows, :], acc[part, 2 * half + 1, rows, :])

    greet([mate, beyond, *in_y, *in_col, *corners], lambda: acc_sides(1))

    first_y = [links.start(strip.at[1], strip_up, down)]
    for a, b in zip(ends, (pl.ds(W, 8), pl.ds(2 * W - 8, 8))):
        first_y.append(links.start(acc.at[:, :, b, :], from_up.at[:, :, a, :], down))
    mine = pl.multiple_of(core * 512, 512)
    other = pl.multiple_of(512 - core * 512, 512)
    halves = links.start(pacc.at[pl.ds(other, 512), :], p1, mate)
    high, low = pieces(SPILL), pieces(SPILL, W)
    y_far = [links.copy(acc.at[:, far, b, :], from_up.at[:, far, a, :], down) for a, b in zip(high, low)]
    y_near = [links.copy(acc.at[:, near, b, :], from_up.at[:, near, a, :], down) for a, b in zip(high, low)]
    y_far[0].start()
    y_far[1].start()
    acc_sides(0)
    old_sides = [sides_of(ext_old[part, 0, pl.ds(0, W), :], ext_old[part, 1, pl.ds(0, W), :]) for part in range(2)]

    def join(rows):
        for part in range(2):
            for t in range(2):
                onward[part, t, rows, :] = acc[part, 2 + t, rows, :] + from_up[part, 2 + t, rows, :]

    def step_rows(rows, to):
        for part in range(2):
            for t in range(2):
                total = acc[part, t, rows, :] + from_up[part, t, rows, :] + from_west[part, t, rows, :]
                frame[part, 1 + t, to, :] = ext_old[part, t, rows, :] + total * (1.0 / 16.0)

    def over(bounds, k, size, work):
        def one(i, _):
            work(pl.multiple_of(i * size, size))
            return 0

        lax.fori_loop(bounds[k] // size, bounds[k + 1] // size, one, 0)

    x_copies = []

    def pass_on(k):
        y_far[k].wait_recv()
        over(SPILL, k, 8, lambda o: join(pl.ds(o, 8)))
        rows = pieces(SPILL)[k]
        x_copies.append(links.start(onward.at[:, :, rows, :], from_west.at[:, :, rows, :], east))

    for copy in first_y:
        copy.wait_recv()
    for a in ends:
        join(a)
    for part in range(2):
        strip_on[part, :, :] = strip[0, part, 1, :, :] + strip_up[part, 1, :, :]
    first_x = [links.start(strip_on, strip_west, east)]
    for a in ends:
        first_x.append(links.start(onward.at[:, :, a, :], from_west.at[:, :, a, :], east))

    halves.wait_recv()

    def join_half(i, _):
        o = pl.multiple_of(i * 64, 64)
        h1[pl.ds(o, 64), :] = pacc[pl.ds(mine + o, 64), :] + p1[pl.ds(o, 64), :]
        return 0

    lax.fori_loop(0, 8, join_half, 0)
    over_col = []
    for d in range(1, COLS):
        block = pl.multiple_of(lax.rem(col + d, COLS) * 32, 32)
        over_col.append(links.start(h1.at[pl.ds(block, 32), :], p2.at[d - 1], in_col[d - 1]))
    y_far[1].wait_send()
    y_far[2].start()
    y_near[0].start()
    pass_on(0)

    for copy in first_x:
        copy.wait_recv()
    for part in range(2):
        total = strip[0, part, 0, :, :] + strip_up[part, 0, :, :] + strip_west[part, :, :]
        strip_new[part, :, :] = old_sides[part] + total * (1.0 / 16.0)
    step_rows(ends[0], pl.ds(TOP, 8))
    step_rows(ends[1], pl.ds(TOP + W - 8, 8))
    top_in, top_out = pl.ds(TOP - 8, 8), pl.ds(TOP, 8)
    low_in, low_out = pl.ds(TOP + W, 8), pl.ds(TOP + W - 8, 8)
    both = pl.ds(1, 2)
    rims = [
        links.start(strip_new.at[:, pl.ds(0, 8), :], rim_in.at[0], west),
        links.start(strip_new.at[:, pl.ds(8, 8), :], rim_in.at[1], east),
        links.start(frame.at[:, both, top_out, :], frame.at[:, both, low_in, :], up),
        links.start(frame.at[:, both, low_out, :], frame.at[:, both, top_in, :], down),
        links.start(frame.at[:, 1, top_out, :], corner_in.at[0], corners[0]),
        links.start(frame.at[:, 2, top_out, :], corner_in.at[1], corners[1]),
        links.start(frame.at[:, 1, low_out, :], corner_in.at[2], corners[2]),
        links.start(frame.at[:, 2, low_out, :], corner_in.at[3], corners[3]),
    ]
    y_far[2].wait_send()
    y_far[3].start()
    y_near[1].start()
    pass_on(1)
    pass_on(2)
    y_near[2].start()
    for copy in over_col:
        copy.wait_recv()
    here = pl.multiple_of(col * 32, 32)
    total = h1[pl.ds(here, 32), :]
    for d in range(COLS - 1):
        total = total + p2[d]
    h3[...] = total
    over_y = [links.start(h3, p4.at[y], to) for to in in_y]
    p4[y] = total

    for copy in rims:
        copy.wait_recv()
    blank = jnp.zeros((LANE - 16, W), F32)
    lane8 = lax.broadcasted_iota(jnp.int32, (8, LANE), 1)
    for part in range(2):
        right_rim = jnp.where(col < COLS - 1, rim_in[0, part, :, :], 0.0)
        left_rim = jnp.where(col > 0, rim_in[1, part, :, :], 0.0)
        frame[part, 0, pl.ds(TOP, W), :] = jnp.concatenate([right_rim, blank, left_rim], axis=0).T
        for on, rows, right, left in ((row > 0, top_in, 2, 3), (row < ROWS - 1, low_in, 0, 1)):
            right_end = jnp.where(col < COLS - 1, corner_in[right, part, :, :], 0.0)
            left_end = jnp.where(col > 0, corner_in[left, part, :, :], 0.0)
            ends_in = jnp.where(lane8 < 8, right_end, jnp.where(lane8 >= LANE - 8, left_end, 0.0))
            frame[part, 0, rows, :] = jnp.where(on, ends_in, 0.0)
            for t in range(1, 3):
                frame[part, t, rows, :] = jnp.where(on, frame[part, t, rows, :], 0.0)
        for t in range(3):
            frame[part, t, pl.ds(0, 8), :] = jnp.zeros((8, LANE), F32)
            frame[part, t, pl.ds(FRAME - 8, 8), :] = jnp.zeros((8, LANE), F32)

    west_on = (col > 0).astype(F32)
    east_on = (col < COLS - 1).astype(F32)
    lane16 = lax.broadcasted_iota(jnp.int32, (16, LANE), 1)
    lane32 = lax.broadcasted_iota(jnp.int32, (32, LANE), 1)

    def tap(ref):
        return lambda a, b: ref[a, step, b]

    def first(o, count, lane, keep):
        parts = correlate_block(lambda t, at: frame[1, t, pl.ds(at, count), :], o, tap(kernel_first), range(3), lane)
        for t in range(3):
            value = frame[0, t, pl.ds(o, count), :] + jnp.tanh(parts[t])
            if t == 0:
                value = value * jnp.where(lane < LANE // 2, east_on, west_on)
            if keep is not None:
                value = value * keep
            real[t, pl.ds(o, count), :] = value

    first(TOP - 8, 8, lane8, (row > 0).astype(F32))
    first(TOP + W, 8, lane8, (row < ROWS - 1).astype(F32))

    def second(o):
        at = pl.ds(o, 32)
        o = o + TOP
        parts = correlate_block(lambda t, a: real[t, pl.ds(a, 32), :], o, tap(kernel_second), range(1, 3), lane32)
        for t in range(2):
            new_re = real[1 + t, pl.ds(o, 32), :]
            new_im = frame[1, 1 + t, pl.ds(o, 32), :] + jnp.tanh(parts[t])
            if last:
                ext[0, at, t * LANE : (t + 1) * LANE] = new_re
                ext[1, at, t * LANE : (t + 1) * LANE] = new_im
            else:
                ext[0, t, at, :] = new_re
                ext[1, t, at, :] = new_im

    if not last:
        copies = halo_copies(links, ext, LATER, west, up)

    def settle(k):
        y_near[k].wait_recv()
        x_copies[k].wait_recv()
        over(SPILL, k, 8, lambda o: step_rows(pl.ds(o, 8), pl.ds(o + TOP, 8)))
        over(REAL, k, 16, lambda o: first(o + TOP, 16, lane16, None))
        over(LATER, k, 32, second)
        if not last:
            copies[0][k].start()
            copies[1][k].start()

    for copy in over_y:
        copy.wait_recv()
    piece = pl.multiple_of(core * 512 + col * 32, 32)
    total = p4[0] + p4[1] + p4[2] + p4[3]
    flat[pl.ds(piece, 32), :] = flat_old[pl.ds(piece, 32), :] + total * (2.0 / math.sqrt(2048.0))

    def gather(first, count, targets):
        rows = pl.ds(first, count)
        return [links.start(flat.at[rows, :], flat.at[rows, :], to) for to in targets]

    back = gather(piece, 32, in_col)

    settle(0)
    pass_on(3)
    y_near[3].start()
    settle(1)
    settle(2)
    for copy in back:
        copy.wait_recv()
    back = gather(mine, 512, [mate])
    settle(3)
    if not last:
        for k in range(0, 2):
            copies[0][k].wait_recv()
            copies[2][k].start()
    if not last:
        for k in range(2, 4):
            copies[0][k].wait_recv()
            copies[2][k].start()
    if not last:
        for copy in [*copies[1], *copies[2]]:
            copy.wait_recv()
    back[0].wait_recv()
    links.drain()


def update_call(step, last, acc, ext, pacc, flat, kernel_first, kernel_second):
    return pl.pallas_call(
        functools.partial(update_kernel, step, last),
        out_shape=(TILE if last else EXT, FLAT),
        in_specs=[VM, VM, VM, VM, SM, SM],
        out_specs=(VM, VM),
        scratch_shapes=[
            pltpu.VMEM((2, 4, W, LANE), F32),
            pltpu.VMEM((2, 2, W, LANE), F32),
            pltpu.VMEM((2, 2, W, LANE), F32),
            pltpu.VMEM((2, 2, 2, 16, W), F32),
            pltpu.VMEM((2, 2, 16, W), F32),
            pltpu.VMEM((2, 16, W), F32),
            pltpu.VMEM((2, 16, W), F32),
            pltpu.VMEM((2, 16, W), F32),
            pltpu.VMEM((2, 2, 8, W), F32),
            pltpu.VMEM((4, 2, 8, LANE), F32),
            pltpu.VMEM((2, 3, FRAME, LANE), F32),
            pltpu.VMEM((3, FRAME, LANE), F32),
            pltpu.VMEM((512, LANE), F32),
            pltpu.VMEM((512, LANE), F32),
            pltpu.VMEM((COLS - 1, 32, LANE), F32),
            pltpu.VMEM((32, LANE), F32),
            pltpu.VMEM((4, 32, LANE), F32),
            DMA((UPDATE_SEMS,)),
            DMA((UPDATE_SEMS,)),
        ],
        compiler_params=pltpu.CompilerParams(
            collective_id=2 if last else 1, has_side_effects=True, vmem_limit_bytes=VLIM
        ),
        name="last_update" if last else "update",
    )(acc, ext, pacc, flat, kernel_first, kernel_second)


def deliver_kernel(tile, flat, obj_out, probe_out, sems):
    copies = [pltpu.make_async_copy(tile, obj_out, sems.at[4])]
    for part in range(2):
        for t in range(2):
            n = part * 2 + t
            copies.append(
                pltpu.make_async_copy(
                    flat.at[pl.ds(n * W, W), :], probe_out.at[part, :, pl.ds(t * LANE, LANE)], sems.at[n]
                )
            )
    for copy in copies:
        copy.start()
    for copy in copies:
        copy.wait()


def deliver_call(tile, flat):
    return pl.pallas_call(
        deliver_kernel,
        out_shape=(TILE, TILE),
        in_specs=[VM, VM],
        out_specs=(HBM, HBM),
        scratch_shapes=[DMA((5,))],
        compiler_params=pltpu.CompilerParams(vmem_limit_bytes=VLIM),
        name="deliver",
    )(tile, flat)


def body(object_field, probe, positions, amplitudes, live, kernel_first, kernel_second):
    ltab, rtab, tab = (jnp.asarray(table) for table in dft_tables())
    places = positions.T
    kernel_first = kernel_first.transpose(1, 0, 2)
    kernel_second = kernel_second.transpose(1, 0, 2)
    iters = kernel_first.shape[1]
    ext, flat, amps = halo_call(object_field, probe, amplitudes)
    for step in range(iters):
        acc, pacc = window_call(places, live, ext, flat, amps, ltab, rtab, tab)
        ext, flat = update_call(step, step == iters - 1, acc, ext, pacc, flat, kernel_first, kernel_second)
    return deliver_call(ext, flat)


def solution(mesh):
    return jax.shard_map(
        body,
        mesh=mesh,
        in_specs=(
            P(None, "row", "col"),
            P(),
            P(("row", "col"), None),
            P(("row", "col"), None, None),
            P(("row", "col")),
            P(),
            P(),
        ),
        out_specs=(P(None, "row", "col"), P()),
        check_vma=False,
    )
```
